32 devices in a mesh: comp: 4 (over y, x), dom: 8 (over z, core).
Axes of the slice: x: 2, y: 2, z: 4, core: 2. Of those that a mesh axis runs over, the one named last changes fastest.
Arguments:
- atm_state: float32 [4, 4, 128, 16, 1024], P('comp', None, None, None, 'dom'), may hold values from -6 to 6
- elem_nbr: int32 [4, 4, 1024], P('comp', None, 'dom'), may hold values from 0 to 3071, as said below
- elem_metric: float32 [4, 16, 1024], P('comp', None, 'dom'), may hold values from 0.02 to 0.2
- bulk_coef: float32 [4, 16, 1024], P('comp', None, 'dom'), may hold values from 0.2 to 2
- stiffness: float32 [16, 16], replicated, may hold values from -1.5 to 1.5
- coupling: float32 [4, 16, 16], replicated, may hold values from -1.5 to 1.5
- atm_vertical: float32 [128, 128], replicated, may hold values from -0.25 to 0.25
- ocean_state: float32 [4, 4, 80, 8192], P('comp', None, None, 'dom'), may hold values from -6 to 6
- cell_nbr: int32 [4, 6, 8192], P('comp', None, 'dom'), may hold values from 0 to 8191, as said below
- cell_diff: float32 [4, 6, 8192], P('comp', None, 'dom'), may hold values from 0.01 to 0.12
- ocean_vertical: float32 [80, 80], replicated, may hold values from -0.3125 to 0.3125
- sea_mask: int32 [4, 8192], P('comp', 'dom'), may hold values 0 or 1
- pair_owner: int32 [4, 256, 1], P('comp', 'dom'), may hold values from 0 to 7, as said below
- pair_block: int32 [4, 256], P('comp', 'dom'), may hold values from 0 to 7
- pair_src: int32 [4, 256], P('comp', 'dom'), may hold values from 0 to 15
- remap_weight: float32 [4, 256, 128, 128], P('comp', 'dom'), may hold values from -0.5 to 0.5
Outputs:
- atm_next: float32 [4, 4, 128, 16, 1024], P('comp', None, None, None, 'dom')
- ocean_next: float32 [4, 4, 80, 8192], P('comp', None, None, 'dom')
The draws below stay inside these ranges and needn't reach their ends.
Inputs may be any that keep to these rules, and one draw needn't show every extreme that they name: `elem_nbr`: each entry of the slabs c < 3 differs from its own element index c * 1024 + e by 1 to 8; the last slab repeats the first. `cell_nbr`: each entry differs from its own cell index by 1 to 128; all slabs are equal. `pair_owner`: within the rows of one device (aligned blocks of 32 rows) no owner is named by more than 8 rows; the owners one below and one above that device's index of dom (counted round) are each named by exactly 8 rows.
All inputs are finite; a program needn't handle non-finite values. No bound on the sum of `sea_mask` on one device may be relied on, other than what follows from the above.
Results may differ from the reference program's by a relative error of at most 0.0001.
Values sent between devices are 32-bit elements; how exact they have to be, the bound alone decides.
No kernel may reach another device: no remote copies, remote signals or barrier semaphores. Data moves between devices by JAX's collectives and lax.ppermute only.
A program may use at most 128 MiB of HBM per device.

```python
import math
import jax
import jax.numpy as jnp
from jax import lax

FIELDS = 4
LEV = 128
NPTS = 16
E_DEV = 128
RIM = 8
BLK = 128
OLEV = 80
HALO_O = 128
NBR_O = 6
PAIRS_DEV = 32
CAP = 8
COMPS = 4
NE = 1024
ATM_ELEMS = 3072
NC = 8192
SRC_BLOCKS = 16
OC_BLOCKS = 8
N_DOM = 8


def neighbour_table(key, count, total, reach):
    first, second = jax.random.split(key)
    own = jnp.arange(total, dtype=jnp.int32)[None, :]
    offset = jax.random.randint(first, (count, total), 1, reach + 1).astype(jnp.int32)
    offset = offset * (jax.random.randint(second, (count, total), 0, 2).astype(jnp.int32) * 2 - 1)
    raw = own + offset
    outside = (raw < 0) | (raw >= total)
    return jnp.where(outside, own - offset, raw).astype(jnp.int32)


def draw_elem_nbr(key, part):
    table = neighbour_table(jax.random.fold_in(key, 11), 4, ATM_ELEMS, RIM)
    slabs = jnp.transpose(table.reshape(4, COMPS - 1, NE), (1, 0, 2))
    return jnp.concatenate([slabs, slabs[:1]], axis=0)


def draw_cell_nbr(key, part):
    table = neighbour_table(jax.random.fold_in(key, 23), NBR_O, NC, HALO_O)
    return jnp.broadcast_to(table[None], (COMPS, NBR_O, NC))


def draw_pair_owner(key, part):
    base = jax.random.fold_in(key, 31)
    spare = (N_DOM - 2) * CAP

    def one_group(group_id):
        group_key = jax.random.fold_in(base, group_id)
        first, second = jax.random.split(group_key)
        home = group_id % N_DOM
        below = jnp.full((CAP,), (home - 1 + N_DOM) % N_DOM, jnp.int32)
        above = jnp.full((CAP,), (home + 1) % N_DOM, jnp.int32)
        step_away = (2 + jnp.arange(spare, dtype=jnp.int32) // CAP) % (N_DOM - 1)
        others = ((home + step_away) % N_DOM).astype(jnp.int32)
        picked = jnp.take(others, jax.random.permutation(first, spare))[:PAIRS_DEV - 2 * CAP]
        rows = jnp.concatenate([below, above, picked]).astype(jnp.int32)
        return jnp.take(rows, jax.random.permutation(second, PAIRS_DEV)).astype(jnp.int32)
    table = jax.vmap(one_group)(jnp.arange(COMPS * N_DOM, dtype=jnp.int32))
    return table.reshape(COMPS, N_DOM * PAIRS_DEV, 1).astype(jnp.int32)


def with_ends(values, own_key, least, top_value):
    index_at = [jax.random.randint(jax.random.fold_in(own_key, axis), (), 0, length) for axis, length in enumerate(values.shape)]
    longest = values.shape.index(max(values.shape))
    neighbour = index_at[:longest] + [(index_at[longest] + 1) % values.shape[longest]] + index_at[longest + 1:]
    return values.at[tuple(index_at)].set(least).at[tuple(neighbour)].set(top_value)


def steps_of(own_key, dims, shards, smallest, high):
    factor_of, own = 1.0, jax.random.fold_in(own_key, 6)
    for position, shards_of in shards:
        draws = jnp.exp(jax.random.uniform(jax.random.fold_in(own, position), (shards_of,), jnp.float32, smallest / len(shards), high / len(shards)))
        factor_of = factor_of * jnp.repeat(draws, dims[position] // shards_of).reshape([-1 if axis == position else 1 for axis in range(len(dims))])
    return factor_of


def scatter_about(rng, dims, deviation, most, pieces=(), kind=jnp.bfloat16):
    drawn = deviation * jax.random.normal(rng, dims, jnp.float32)
    if pieces:
        drawn = drawn * steps_of(rng, dims, pieces, -0.22, 0.18)
    return jnp.clip(drawn, -most, most).astype(kind)


def setup_inputs(seed: int = 0) -> dict:
    streams_of = jax.random.split(jax.random.key(seed), 17)
    return {
        "atm_state": scatter_about(streams_of[0], (COMPS, FIELDS, LEV, NPTS, NE), 1.0, 6.0, ((0, 4), (4, 8)), jnp.float32),
        "elem_nbr": draw_elem_nbr(jax.random.fold_in(streams_of[16], 71), 0),
        "elem_metric": jnp.clip(jnp.exp(math.log(0.2) - 2.3025851 * jax.random.uniform(streams_of[2], (COMPS, NPTS, NE), jnp.float32) ** steps_of(streams_of[2], (COMPS, NPTS, NE), ((0, 4), (2, 8)), -0.2, 0.2)), 0.02, 0.2),
        "bulk_coef": jnp.clip(jnp.exp(math.log(2.0) - 2.3025851 * jax.random.uniform(streams_of[3], (COMPS, NPTS, NE), jnp.float32) ** steps_of(streams_of[3], (COMPS, NPTS, NE), ((0, 4), (2, 8)), -0.2, 0.2)), 0.2, 2.0),
        "stiffness": scatter_about(streams_of[4], (NPTS, NPTS), NPTS ** -0.5, 1.5, (), jnp.float32),
        "coupling": scatter_about(streams_of[5], (4, NPTS, NPTS), NPTS ** -0.5, 1.5, (), jnp.float32),
        "atm_vertical": scatter_about(streams_of[6], (LEV, LEV), (4 * LEV) ** -0.5, 0.25, (), jnp.float32),
        "ocean_state": scatter_about(streams_of[7], (COMPS, FIELDS, OLEV, NC), 1.0, 6.0, ((0, 4), (3, 8)), jnp.float32),
        "cell_nbr": draw_cell_nbr(jax.random.fold_in(streams_of[16], 71), 0),
        "cell_diff": jnp.clip(jnp.exp(math.log(0.12) - 2.4849066 * jax.random.uniform(streams_of[9], (COMPS, NBR_O, NC), jnp.float32) ** steps_of(streams_of[9], (COMPS, NBR_O, NC), ((0, 4), (2, 8)), -0.2, 0.2)), 0.01, 0.12),
        "ocean_vertical": scatter_about(streams_of[10], (OLEV, OLEV), (4 * OLEV) ** -0.5, 0.3125, (), jnp.float32),
        "sea_mask": with_ends((jax.random.randint(streams_of[11], (COMPS, NC), 0, 4) < 3).astype(jnp.int32), jax.random.fold_in(streams_of[11], 1), 0, 1),
        "pair_owner": draw_pair_owner(jax.random.fold_in(streams_of[16], 71), 0),
        "pair_block": with_ends(jax.random.randint(streams_of[13], (COMPS, N_DOM * PAIRS_DEV), 0, OC_BLOCKS), jax.random.fold_in(streams_of[13], 1), 0, OC_BLOCKS - 1).astype(jnp.int32),
        "pair_src": with_ends(jax.random.randint(streams_of[14], (COMPS, N_DOM * PAIRS_DEV), 0, SRC_BLOCKS), jax.random.fold_in(streams_of[14], 1), 0, SRC_BLOCKS - 1).astype(jnp.int32),
        "remap_weight": scatter_about(streams_of[15], (COMPS, N_DOM * PAIRS_DEV, BLK, BLK), BLK ** -0.5, 0.5, ((0, 4), (1, 8)), jnp.float32),
    }


highest = lax.Precision.HIGHEST


def reference(atm_state, elem_nbr, elem_metric, bulk_coef, stiffness, coupling, atm_vertical, ocean_state, cell_nbr, cell_diff, ocean_vertical, sea_mask, pair_owner, pair_block, pair_src, remap_weight):
    live = COMPS - 1
    fields = atm_state.shape[1]
    levels = atm_state.shape[2]
    points = atm_state.shape[3]
    state = jnp.transpose(atm_state[:live], (1, 2, 3, 0, 4)).reshape(fields, levels, points, ATM_ELEMS)
    metric = jnp.transpose(elem_metric[:live], (1, 0, 2)).reshape(points, ATM_ELEMS)
    coef = jnp.transpose(bulk_coef[:live], (1, 0, 2)).reshape(points, ATM_ELEMS)
    neighbours = jnp.transpose(elem_nbr[:live], (1, 0, 2)).reshape(4, ATM_ELEMS)
    ocean = ocean_state[COMPS - 1]
    cell_table = cell_nbr[COMPS - 1]
    diffusion = cell_diff[COMPS - 1]
    sea = sea_mask[COMPS - 1]
    owner = pair_owner[:live, :, 0].reshape(-1)
    target = (owner * OC_BLOCKS + pair_block[:live].reshape(-1)).astype(jnp.int32)
    source = pair_src[:live].reshape(-1)
    weights = remap_weight[:live].reshape(-1, BLK, BLK)
    group = (jnp.arange(owner.shape[0], dtype=jnp.int32) // PAIRS_DEV).astype(jnp.int32)
    per_row = E_DEV // BLK
    point_of = (source // per_row).astype(jnp.int32)
    block_of = (group * per_row + source % per_row).astype(jnp.int32)
    atm_blocks = ATM_ELEMS // BLK
    top = ocean[:, 0, :].reshape(fields, NC // BLK, BLK)
    picked = top[:, target, :]
    contrib = jnp.einsum("fpo,pao->fpa", picked, weights, precision=highest)
    surface = jnp.zeros((fields, points, atm_blocks, BLK), jnp.float32)
    surface = surface.at[:, point_of, block_of].add(contrib).reshape(fields, points, ATM_ELEMS)
    flux = coef[None] * (state[:, levels - 1] - surface)
    flux_blocks = flux.reshape(fields, points, atm_blocks, BLK)[:, point_of, block_of]
    sent = jnp.einsum("fpa,pao->fpo", flux_blocks, weights, precision=highest)
    oflux = jnp.zeros((fields, NC // BLK, BLK), jnp.float32).at[:, target].add(sent).reshape(fields, NC)
    for step in range(2):
        tend = jnp.einsum("pq,flqe->flpe", stiffness, state, precision=highest)
        tend = tend + jnp.einsum("lm,fmpe->flpe", atm_vertical, state, precision=highest)
        for side in range(4):
            beside = jnp.take(state, neighbours[side], axis=3)
            tend = tend + jnp.einsum("pq,flqe->flpe", coupling[side], beside, precision=highest)
        state = state + metric[None, None] * tend
        state = state.at[:, levels - 1].add(-0.5 * flux)
    lap = jnp.zeros_like(ocean)
    for side in range(cell_table.shape[0]):
        lap = lap + diffusion[side][None, None] * (jnp.take(ocean, cell_table[side], axis=2) - ocean)
    fresh = ocean + lap + jnp.einsum("lm,fmc->flc", ocean_vertical, ocean, precision=highest)
    fresh = fresh.at[:, 0].add(0.5 * oflux)
    fresh = jnp.where(sea[None, None] == 1, fresh, ocean)
    atm_part = jnp.transpose(state.reshape(fields, levels, points, live, NE), (3, 0, 1, 2, 4))
    atm_next = jnp.concatenate([atm_part, jnp.zeros((1, fields, levels, points, NE), jnp.float32)], axis=0)
    ocean_next = jnp.concatenate([jnp.zeros((live,) + ocean.shape, jnp.float32), fresh[None]], axis=0)
    return (atm_next, ocean_next)
```

```python
import functools

import jax
import jax.numpy as jnp
from jax import lax
from jax.experimental import pallas as pl
from jax.experimental.pallas import tpu as pltpu
from jax.sharding import PartitionSpec as P

RIM = 8
BLK = 128
HALO_O = 128
LANES = 128
GROUP = 8

F32 = jnp.float32
BF16 = jnp.bfloat16
VMEM_LIMIT = 56 * 1024 * 1024
ANY = pl.BlockSpec(memory_space=pl.ANY)
SMEM = pl.BlockSpec(memory_space=pltpu.SMEM)
VMEM = pl.BlockSpec(memory_space=pltpu.VMEM)


def params():
    return pltpu.CompilerParams(vmem_limit_bytes=VMEM_LIMIT)


def cost(flops, moved):
    return pl.CostEstimate(flops=flops, bytes_accessed=moved, transcendentals=0)


def split(x):
    hi = x.astype(BF16)
    return hi, (x - hi.astype(F32)).astype(BF16)


def dot(a, b):
    return jnp.dot(a, b, preferred_element_type=F32)


def dot_t(a, b):
    return lax.dot_general(a, b, (((1,), (1,)), ((), ())), preferred_element_type=F32)


def turned(rows):
    n = rows.shape[0]
    if n < LANES:
        rows = jnp.concatenate([rows, jnp.zeros((LANES - n, LANES), rows.dtype)], axis=0)
    return rows.T


def turn_kernel(flag, x, o, xt, up, down, xv, tv, in_sem, out_sem, halo_sem):
    fields, points = xv.shape[0], 16
    rows = tv.shape[1]
    olev, cells = o.shape[1], o.shape[2]

    @pl.when(flag[0] == 0)
    def _():
        loads = [pltpu.make_async_copy(x.at[f], xv.at[f], in_sem.at[f]) for f in range(fields)]
        for load in loads:
            load.start()
        for f in range(fields):
            loads[f].wait()
            for q in range(points):
                t = xv[f, pl.ds(q, LANES, stride=points), :].T
                for g in range(LANES // GROUP):
                    tv[f, pl.ds(g * GROUP * points + q * GROUP, GROUP), :] = t[g * GROUP : (g + 1) * GROUP]
            pltpu.make_async_copy(tv.at[f, pl.ds(rows - LANES, LANES)], up.at[f], halo_sem.at[0, f]).start()
            pltpu.make_async_copy(tv.at[f, pl.ds(0, LANES)], down.at[f], halo_sem.at[1, f]).start()
            pltpu.make_async_copy(tv.at[f], xt.at[f], out_sem.at[f]).start()
        for f in range(fields):
            pltpu.make_async_copy(tv.at[f, pl.ds(rows - LANES, LANES)], up.at[f], halo_sem.at[0, f]).wait()
            pltpu.make_async_copy(tv.at[f, pl.ds(0, LANES)], down.at[f], halo_sem.at[1, f]).wait()
            pltpu.make_async_copy(tv.at[f], xt.at[f], out_sem.at[f]).wait()

    @pl.when(flag[0] != 0)
    def _():
        copies = []
        for f in range(fields):
            copies.append(
                pltpu.make_async_copy(
                    o.at[f, :, pl.ds(cells - HALO_O, HALO_O)], up.at[f, pl.ds(0, olev)], halo_sem.at[0, f]
                )
            )
            copies.append(
                pltpu.make_async_copy(o.at[f, :, pl.ds(0, HALO_O)], down.at[f, pl.ds(0, olev)], halo_sem.at[1, f])
            )
        for copy in copies:
            copy.start()
        for copy in copies:
            copy.wait()


def turn(flag, state, ocean):
    fields, levels, points, elems = state.shape
    rows = points * elems
    return pl.pallas_call(
        turn_kernel,
        out_shape=(
            jax.ShapeDtypeStruct((fields, rows, levels), F32),
            jax.ShapeDtypeStruct((fields, LANES, LANES), F32),
            jax.ShapeDtypeStruct((fields, LANES, LANES), F32),
        ),
        in_specs=[SMEM, ANY, ANY],
        out_specs=(ANY, ANY, ANY),
        scratch_shapes=[
            pltpu.VMEM((fields, levels * points, elems), F32),
            pltpu.VMEM((fields, rows, levels), F32),
            pltpu.SemaphoreType.DMA((fields,)),
            pltpu.SemaphoreType.DMA((fields,)),
            pltpu.SemaphoreType.DMA((2, fields)),
        ],
        compiler_params=params(),
        cost_estimate=cost(0, 9 << 20),
        name="turn_state",
    )(flag, state.reshape(fields, levels * points, elems), ocean)


def table_kernel(flag, base, nbr, ops, hi, lo, nt, cx):
    block = pl.program_id(0)
    points = ops.shape[1]
    sides = nbr.shape[0]

    @pl.when(flag[0] == 0)
    def _():
        @pl.when(block == 0)
        def _():
            nt[...] = turned((nbr[...] - base[0]).astype(F32))
            spread = lax.broadcasted_iota(jnp.int32, (points, LANES), 1) // GROUP
            spread = (spread == lax.broadcasted_iota(jnp.int32, (points, LANES), 0)).astype(F32)
            cx[...] = lax.dot_general(
                ops[...],
                spread,
                (((1,), (0,)), ((), ())),
                precision=lax.Precision.HIGHEST,
                preferred_element_type=F32,
            )

        lane = lax.broadcasted_iota(jnp.int32, (GROUP, LANES), 1) % GROUP
        lane_f = lane.astype(F32)
        same = lane == lax.broadcasted_iota(jnp.int32, (GROUP, LANES), 0)
        for g in range(2):
            first = pl.multiple_of(block * 2 * GROUP + g * GROUP, GROUP)
            own = nt[pl.ds(first, GROUP), :]
            for h in range(4):
                cols = pl.ds(h * LANES, LANES)
                if h - g not in (0, 1, 2):
                    zero = jnp.zeros((LANES, LANES), BF16)
                    hi[0, pl.ds(g * LANES, LANES), cols] = zero
                    lo[0, pl.ds(g * LANES, LANES), cols] = zero
                    continue
                start = (block * 2 * GROUP + (h - 1) * GROUP).astype(F32)
                masks = [
                    jnp.broadcast_to(own[:, s : s + 1], (GROUP, LANES)) - start == lane_f for s in range(sides)
                ]
                for p in range(0, points, 2):
                    pair = []
                    for pp in (p, p + 1):
                        total = jnp.zeros((GROUP, LANES), F32)
                        for s in range(sides):
                            row = jnp.broadcast_to(cx[pl.ds(s * points + pp, 1), :], (GROUP, LANES))
                            total = total + jnp.where(masks[s], row, 0.0)
                        if h == g + 1:
                            row = jnp.broadcast_to(cx[pl.ds(sides * points + pp, 1), :], (GROUP, LANES))
                            total = total + jnp.where(same, row, 0.0)
                        pair.append(total)
                    top, rest = split(jnp.concatenate(pair, axis=0))
                    at = pl.ds(g * LANES + p * GROUP, 2 * GROUP)
                    hi[0, at, cols] = top
                    lo[0, at, cols] = rest


def tables(flag, base, nbr, ops, points):
    blocks = nbr.shape[1] // (2 * GROUP)
    shape = jax.ShapeDtypeStruct((blocks, 2 * LANES, 4 * LANES), BF16)
    out = pl.BlockSpec((1, 2 * LANES, 4 * LANES), lambda b: (b, 0, 0))
    return pl.pallas_call(
        table_kernel,
        grid=(blocks,),
        out_shape=(shape, shape),
        in_specs=[SMEM, SMEM, VMEM, VMEM],
        out_specs=(out, out),
        scratch_shapes=[pltpu.VMEM((LANES, LANES), F32), pltpu.VMEM((ops.shape[0], LANES), F32)],
        compiler_params=params(),
        cost_estimate=cost(0, 4 << 20),
        name="neighbour_tables",
    )(flag, base, nbr, ops)


def put_split(xhl, at, f, fields, x):
    hi, lo = split(x)
    xhl[at, pl.ds(f * LANES, LANES)] = hi
    xhl[at, pl.ds((fields + f) * LANES, LANES)] = lo


def advance(b, xv, xhl, thi, tlo, wa, mb, store):
    fields = xv.shape[0]
    width = fields * LANES
    first = pl.multiple_of(b * 2 * LANES, 2 * LANES)
    window = pl.ds(first, 4 * LANES)
    both = dot(thi[b], xhl[window, :])
    rest = dot(tlo[b], xhl[window, pl.ds(0, width)])
    rows = pl.ds(first, 2 * LANES)
    inner = pl.ds(pl.multiple_of(first + LANES, LANES), 2 * LANES)
    m = mb[rows, :]
    for f in range(fields):
        lo_at = slice((fields + f) * LANES, (fields + f + 1) * LANES)
        hi_at = slice(f * LANES, (f + 1) * LANES)
        pair = jnp.concatenate([xhl[inner, hi_at], xhl[inner, lo_at]], axis=1)
        v = dot(pair, wa[...])
        tend = both[:, hi_at] + both[:, lo_at] + rest[:, hi_at] + v[:, :LANES] + v[:, LANES:]
        store(f, rows, xv[f, rows, :] + m * tend)


def prepare(metric, vertical, wa, mb):
    points = metric.shape[0]
    mt = turned(metric[...])
    for g in range(LANES // GROUP):
        for q in range(points):
            mb[pl.ds((g * points + q) * GROUP, GROUP), :] = jnp.broadcast_to(
                mt[g * GROUP : (g + 1) * GROUP, q : q + 1], (GROUP, LANES)
            )
    hi, lo = split(vertical[...].T)
    wa[pl.ds(0, LANES), pl.ds(0, LANES)] = hi
    wa[pl.ds(LANES, LANES), pl.ds(0, LANES)] = hi
    wa[pl.ds(0, LANES), pl.ds(LANES, LANES)] = lo
    wa[pl.ds(LANES, LANES), pl.ds(LANES, LANES)] = jnp.zeros((LANES, LANES), BF16)


def table_copies(thi, tlo, hi_v, lo_v, sem):
    blocks = thi.shape[0]
    out = []
    for b in range(blocks):
        out.append(
            (
                pltpu.make_async_copy(thi.at[b], hi_v.at[b], sem.at[0, b]),
                pltpu.make_async_copy(tlo.at[b], lo_v.at[b], sem.at[1, b]),
            )
        )
    return out


def first_kernel(
    flag, xt, left, right, thi, tlo, metric, vertical, u, edges, xv, xhl, hi_v, lo_v, wa, mb, x_sem, t_sem, u_sem, e_sem
):
    fields, rows = xv.shape[0], xv.shape[1]
    blocks = thi.shape[0]

    @pl.when(flag[0] == 0)
    def _():
        loads = [pltpu.make_async_copy(xt.at[f], xv.at[f], x_sem.at[f]) for f in range(fields)]
        for load in loads:
            load.start()
        table = table_copies(thi, tlo, hi_v, lo_v, t_sem)
        for a, b in table:
            a.start()
            b.start()
        prepare(metric, vertical, wa, mb)
        for f in range(fields):
            put_split(xhl, pl.ds(0, LANES), f, fields, left[f])
            put_split(xhl, pl.ds(rows + LANES, LANES), f, fields, right[f])
        for f in range(fields):
            loads[f].wait()
            for c in range(rows // LANES):
                put_split(xhl, pl.ds((c + 1) * LANES, LANES), f, fields, xv[f, pl.ds(c * LANES, LANES), :])
        for a, b in table:
            a.wait()
            b.wait()

        def store(f, at, value):
            xv[f, at, :] = value

        @pl.loop(0, blocks)
        def _(b):
            advance(b, xv, xhl, hi_v, lo_v, wa, mb, store)

        copies = []
        for f in range(fields):
            copies.append(pltpu.make_async_copy(xv.at[f], u.at[f], u_sem.at[f]))
            copies.append(pltpu.make_async_copy(xv.at[f, pl.ds(0, LANES)], edges.at[0, f], e_sem.at[0, f]))
            copies.append(pltpu.make_async_copy(xv.at[f, pl.ds(rows - LANES, LANES)], edges.at[1, f], e_sem.at[1, f]))
        for copy in copies:
            copy.start()
        for copy in copies:
            copy.wait()


def first_step(flag, xt, left, right, thi, tlo, metric, vertical):
    fields, rows, levels = xt.shape
    blocks = thi.shape[0]
    return pl.pallas_call(
        first_kernel,
        out_shape=(
            jax.ShapeDtypeStruct((fields, rows, levels), F32),
            jax.ShapeDtypeStruct((2, fields, LANES, LANES), F32),
        ),
        in_specs=[SMEM, ANY, VMEM, VMEM, ANY, ANY, VMEM, VMEM],
        out_specs=(ANY, ANY),
        scratch_shapes=[
            pltpu.VMEM((fields, rows, levels), F32),
            pltpu.VMEM((rows + 2 * LANES, 2 * fields * LANES), BF16),
            pltpu.VMEM(thi.shape, BF16),
            pltpu.VMEM(thi.shape, BF16),
            pltpu.VMEM((2 * LANES, 2 * LANES), BF16),
            pltpu.VMEM((rows, LANES), F32),
            pltpu.SemaphoreType.DMA((fields,)),
            pltpu.SemaphoreType.DMA((2, blocks)),
            pltpu.SemaphoreType.DMA((fields,)),
            pltpu.SemaphoreType.DMA((2, fields)),
        ],
        compiler_params=params(),
        cost_estimate=cost(10_000_000_000, 12 << 20),
        name="first_step",
    )(flag, xt, left, right, thi, tlo, metric, vertical)


def flux_kernel(
    flag, owner, block, source, tops, weights, coef, surface_level, edges, flux, sent, down, up, wv, wcat, surf, fl, w_sem
):
    pairs = weights.shape[0]
    points = coef.shape[0]
    fields = surface_level.shape[0]
    ocean_blocks = sent.shape[0] // tops.shape[0]

    @pl.when(flag[0] == 0)
    def _():
        parts = w_sem.shape[0]
        each = pairs // parts
        loads = [
            pltpu.make_async_copy(weights.at[pl.ds(i * each, each)], wv.at[pl.ds(i * each, each)], w_sem.at[i])
            for i in range(parts)
        ]
        for load in loads:
            load.start()
        surf[...] = jnp.zeros_like(surf)
        sent[...] = jnp.zeros_like(sent)

        def doubled(rows):
            hi, lo = split(rows)
            hi, lo = hi.astype(F32), lo.astype(F32)
            eight = jnp.concatenate([hi, lo], axis=0).astype(BF16)
            return jnp.concatenate([eight, eight], axis=1)

        for i in range(parts):
            loads[i].wait()

            @pl.loop(i * each, (i + 1) * each)
            def _(r):
                hi, lo = split(wv[r])
                wcat[r, :, pl.ds(0, BLK)] = hi
                wcat[r, :, pl.ds(BLK, BLK)] = lo

        for r in range(pairs):
            at = pl.multiple_of(block[r] * BLK, BLK)
            rows = doubled(tops[owner[r], :, pl.ds(at, BLK)])
            out = dot_t(rows, wcat[r])
            surf[source[r]] += out[:fields] + out[fields:]

        for p in range(points):
            value = coef[pl.ds(p, 1), :] * (surface_level[:, p, :] - surf[p])
            fl[p] = value
            flux[:, p, :] = value

        for r in range(pairs):
            rows = doubled(fl[source[r]])
            both = jnp.concatenate([wcat[r, :, pl.ds(0, BLK)], wcat[r, :, pl.ds(BLK, BLK)]], axis=0)
            out = dot(rows, both)
            sent[owner[r] * ocean_blocks + block[r]] += out[:fields] + out[fields:]

        lane = lax.broadcasted_iota(jnp.int32, (GROUP, LANES), 1)
        for f in range(fields):
            ft = turned(flux[f])
            for side, out_ref, g in ((0, down, 0), (1, up, LANES // GROUP - 1)):
                for q in range(points):
                    at = pl.ds(q * GROUP, GROUP)
                    column = jnp.broadcast_to(ft[g * GROUP : (g + 1) * GROUP, q : q + 1], (GROUP, LANES))
                    out_ref[f, at, :] = edges[side, f, at, :] - jnp.where(lane == LANES - 1, 0.5 * column, 0.0)


def fluxes(flag, owner, block, source, tops, weights, coef, surface_level, edges, ocean_blocks):
    fields, points, elems = surface_level.shape
    pairs = weights.shape[0]
    owners = tops.shape[0]
    halo = jax.ShapeDtypeStruct((fields, LANES, LANES), F32)
    return pl.pallas_call(
        flux_kernel,
        out_shape=(
            jax.ShapeDtypeStruct((fields, points, elems), F32),
            jax.ShapeDtypeStruct((owners * ocean_blocks, fields, BLK), F32),
            halo,
            halo,
        ),
        in_specs=[SMEM, SMEM, SMEM, SMEM, VMEM, ANY, VMEM, VMEM, VMEM],
        out_specs=(VMEM, VMEM, VMEM, VMEM),
        scratch_shapes=[
            pltpu.VMEM(weights.shape, F32),
            pltpu.VMEM((pairs, BLK, 2 * BLK), BF16),
            pltpu.VMEM((points, fields, BLK), F32),
            pltpu.VMEM((points, fields, BLK), F32),
            pltpu.SemaphoreType.DMA((4,)),
        ],
        compiler_params=params(),
        cost_estimate=cost(1_000_000_000, 4 << 20),
        name="fluxes",
    )(flag, owner, block, source, tops, weights, coef, surface_level, edges)


def second_kernel(
    flag, u, left, right, thi, tlo, metric, vertical, flux, out, xv, xhl, hi_v, lo_v, wa, mb, ov, x_sem, t_sem, o_sem
):
    fields, rows = xv.shape[0], xv.shape[1]
    blocks = thi.shape[0]
    points = metric.shape[0]
    levels = xv.shape[2]

    @pl.when(flag[0] == 0)
    def _():
        loads = [pltpu.make_async_copy(u.at[f], xv.at[f], x_sem.at[f]) for f in range(fields)]
        for load in loads:
            load.start()
        table = table_copies(thi, tlo, hi_v, lo_v, t_sem)
        for a, b in table:
            a.start()
            b.start()
        prepare(metric, vertical, wa, mb)
        for f in range(fields):
            put_split(xhl, pl.ds(0, LANES), f, fields, left[f])
            put_split(xhl, pl.ds(rows + LANES, LANES), f, fields, right[f])
        lane = lax.broadcasted_iota(jnp.int32, (GROUP, LANES), 1)
        for f in range(fields):
            ft = turned(-0.5 * flux[f])
            loads[f].wait()
            for g in range(LANES // GROUP):
                pieces = []
                for q in range(points):
                    column = jnp.broadcast_to(ft[g * GROUP : (g + 1) * GROUP, q : q + 1], (GROUP, LANES))
                    pieces.append(jnp.where(lane == LANES - 1, column, 0.0))
                at = pl.ds(g * LANES, LANES)
                x = xv[f, at, :] + jnp.concatenate(pieces, axis=0)
                xv[f, at, :] = x
                put_split(xhl, pl.ds((g + 1) * LANES, LANES), f, fields, x)
        for a, b in table:
            a.wait()
            b.wait()

        def store(f, at, value):
            xv[f, at, :] = value

        @pl.loop(0, blocks)
        def _(b):
            advance(b, xv, xhl, hi_v, lo_v, wa, mb, store)

        copies = [pltpu.make_async_copy(ov.at[f], out.at[f], o_sem.at[f]) for f in range(fields)]
        for f in range(fields):
            for p in range(points):
                cols = [xv[f, pl.ds(g * LANES + p * GROUP, GROUP), :] for g in range(LANES // GROUP)]
                ov[f, pl.ds(p, LANES, stride=points), :] = jnp.concatenate(cols, axis=0).T
            last = pl.ds((levels - 1) * points, points)
            ov[f, last, :] = ov[f, last, :] - 0.5 * flux[f]
            copies[f].start()
        for copy in copies:
            copy.wait()

    @pl.when(flag[0] != 0)
    def _():
        ov[0] = jnp.zeros_like(ov[0])
        copies = [pltpu.make_async_copy(ov.at[0], out.at[f], o_sem.at[f]) for f in range(fields)]
        for copy in copies:
            copy.start()
        for copy in copies:
            copy.wait()


def second_step(flag, u, left, right, thi, tlo, metric, vertical, flux):
    fields, rows, levels = u.shape
    blocks = thi.shape[0]
    points = metric.shape[0]
    return pl.pallas_call(
        second_kernel,
        out_shape=jax.ShapeDtypeStruct((fields, levels * points, LANES), F32),
        in_specs=[SMEM, ANY, VMEM, VMEM, ANY, ANY, VMEM, VMEM, VMEM],
        out_specs=ANY,
        scratch_shapes=[
            pltpu.VMEM((fields, rows, levels), F32),
            pltpu.VMEM((rows + 2 * LANES, 2 * fields * LANES), BF16),
            pltpu.VMEM(thi.shape, BF16),
            pltpu.VMEM(thi.shape, BF16),
            pltpu.VMEM((2 * LANES, 2 * LANES), BF16),
            pltpu.VMEM((rows, LANES), F32),
            pltpu.VMEM((fields, levels * points, LANES), F32),
            pltpu.SemaphoreType.DMA((fields,)),
            pltpu.SemaphoreType.DMA((2, blocks)),
            pltpu.SemaphoreType.DMA((fields,)),
        ],
        compiler_params=params(),
        cost_estimate=cost(10_000_000_000, 12 << 20),
        name="second_step",
    )(flag, u, left, right, thi, tlo, metric, vertical, flux)


def ocean_kernel(flag, base, o, left, right, nbr, diff, vertical, mask, out, ov, ext, dhi, dlo, res, o_sem, out_sem):
    fields, olev, cells = ov.shape
    sides = nbr.shape[0]
    blocks = cells // LANES

    @pl.when(flag[0] != 0)
    def _():
        load = pltpu.make_async_copy(o, ov, o_sem)
        load.start()
        load.wait()
        for f in range(fields):
            rows = pl.ds(f * olev, olev)
            for at, value in ((0, left[f, :olev, :]), (HALO_O + cells, right[f, :olev, :])):
                hi, lo = split(value)
                ext[0, rows, pl.ds(at, HALO_O)] = hi
                ext[1, rows, pl.ds(at, HALO_O)] = lo
            hi, lo = split(ov[f])
            ext[0, rows, pl.ds(HALO_O, cells)] = hi
            ext[1, rows, pl.ds(HALO_O, cells)] = lo
        vhi, vlo = split(vertical[...])

        @pl.loop(0, blocks)
        def _(b):
            first = pl.multiple_of(b * LANES, LANES)
            here = pl.ds(first, LANES)
            start = base[0] + first - HALO_O
            place = lax.broadcasted_iota(jnp.int32, (3 * LANES, LANES), 0)
            table = jnp.zeros((3 * LANES, LANES), F32)
            held = jnp.zeros((1, LANES), F32)
            for k in range(sides):
                d = diff[pl.ds(k, 1), here]
                held = held + d
                table = table + jnp.where(place == nbr[pl.ds(k, 1), here] - start, d, 0.0)
            hi, lo = split(table)
            window = pl.ds(first, 3 * LANES)
            lap = dot(ext[0, :, window], hi) + dot(ext[1, :, window], hi) + dot(ext[0, :, window], lo)
            inner = pl.ds(pl.multiple_of(first + HALO_O, LANES), LANES)
            sea = mask[:, here] == 1
            for f in range(fields):
                rows = pl.ds(f * olev, olev)
                xhi, xlo = ext[0, rows, inner], ext[1, rows, inner]
                v = dot(vhi, xhi) + dot(vhi, xlo) + dot(vlo, xhi)
                own = ov[f, :, here]
                fresh = own + (lap[f * olev : (f + 1) * olev] - held * own) + v
                res[f, :, here] = jnp.where(sea, fresh, own)

    @pl.when(flag[0] == 0)
    def _():
        res[...] = jnp.zeros_like(res)

    copy = pltpu.make_async_copy(res, out, out_sem)
    copy.start()
    copy.wait()


def ocean_step(flag, base, ocean, left, right, nbr, diff, vertical, mask):
    fields, olev, cells = ocean.shape
    return pl.pallas_call(
        ocean_kernel,
        out_shape=jax.ShapeDtypeStruct(ocean.shape, F32),
        in_specs=[SMEM, SMEM, ANY, VMEM, VMEM, VMEM, VMEM, VMEM, VMEM],
        out_specs=ANY,
        scratch_shapes=[
            pltpu.VMEM(ocean.shape, F32),
            pltpu.VMEM((2, fields * olev, cells + 2 * HALO_O), BF16),
            pltpu.VMEM((8, LANES), BF16),
            pltpu.VMEM((8, LANES), BF16),
            pltpu.VMEM(ocean.shape, F32),
            pltpu.SemaphoreType.DMA,
            pltpu.SemaphoreType.DMA,
        ],
        compiler_params=params(),
        cost_estimate=cost(2_000_000_000, 3 << 20),
        name="ocean_step",
    )(flag, base, ocean, left, right, nbr, diff, vertical, mask)


def finish_kernel(flag, fresh, arrived, mask, out, rows_v, in_sem, out_sem):
    del fresh
    fields, cells = rows_v.shape[0], rows_v.shape[2]
    parts = arrived.shape[0]

    @pl.when(flag[0] != 0)
    def _():
        loads = [
            pltpu.make_async_copy(out.at[f, pl.ds(0, 8)], rows_v.at[f], in_sem.at[f]) for f in range(fields)
        ]
        stores = [
            pltpu.make_async_copy(rows_v.at[f], out.at[f, pl.ds(0, 8)], out_sem.at[f]) for f in range(fields)
        ]
        for load in loads:
            load.start()
        for load in loads:
            load.wait()
        for b in range(cells // BLK):
            here = pl.ds(b * BLK, BLK)
            total = arrived[0, b]
            for i in range(1, parts):
                total = total + arrived[i, b]
            total = jnp.where(mask[:, here] == 1, 0.5 * total, 0.0)
            for f in range(fields):
                rows_v[f, pl.ds(0, 1), here] = rows_v[f, pl.ds(0, 1), here] + total[f : f + 1]
        for store in stores:
            store.start()
        for store in stores:
            store.wait()


def finish(flag, fresh, arrived, mask):
    fields, olev, cells = fresh.shape
    return pl.pallas_call(
        finish_kernel,
        out_shape=jax.ShapeDtypeStruct(fresh.shape, F32),
        in_specs=[SMEM, ANY, VMEM, VMEM],
        out_specs=ANY,
        input_output_aliases={1: 0},
        scratch_shapes=[
            pltpu.VMEM((fields, 8, cells), F32),
            pltpu.SemaphoreType.DMA((fields,)),
            pltpu.SemaphoreType.DMA((fields,)),
        ],
        compiler_params=params(),
        cost_estimate=cost(0, 1 << 18),
        name="finish_ocean",
    )(flag, fresh, arrived, mask)


def local(
    atm_state,
    elem_nbr,
    elem_metric,
    bulk_coef,
    stiffness,
    coupling,
    atm_vertical,
    ocean_state,
    cell_nbr,
    cell_diff,
    ocean_vertical,
    sea_mask,
    pair_owner,
    pair_block,
    pair_src,
    remap_weight,
):
    n_comp = lax.axis_size("comp")
    n_dom = lax.axis_size("dom")
    comp_index = lax.axis_index("comp")
    dom_index = lax.axis_index("dom")
    live = n_comp - 1
    state = atm_state[0]
    ocean = ocean_state[0]
    fields, levels, points, elems = state.shape
    cells = ocean.shape[2]
    ocean_blocks = cells // BLK
    flag = (comp_index == live).astype(jnp.int32).reshape(1)
    joined = (comp_index * n_dom + dom_index) * elems
    elem_base = joined.astype(jnp.int32).reshape(1)
    cell_base = (dom_index * cells).astype(jnp.int32).reshape(1)

    both = ("comp", "dom")
    atm_up = [(i, i + 1) for i in range(live * n_dom - 1)]
    sea_up = [(live * n_dom + i, live * n_dom + i + 1) for i in range(n_dom - 1)]
    going_up = atm_up + sea_up
    going_down = [(j, i) for i, j in going_up]

    def from_ocean(c):
        return [(live * n_dom + d, c * n_dom + d) for d in range(n_dom)]

    def to_ocean(c):
        return [(c * n_dom + d, live * n_dom + d) for d in range(n_dom)]

    top = ocean[:, 0, :]
    got = sum(lax.ppermute(top, both, from_ocean(c)) for c in range(live))
    tops = lax.all_to_all(
        jnp.broadcast_to(got[None], (n_dom,) + got.shape), "dom", split_axis=0, concat_axis=0, tiled=True
    )

    xt, send_up, send_down = turn(flag, state, ocean)
    left = lax.ppermute(send_up, both, going_up)
    right = lax.ppermute(send_down, both, going_down)

    ops = jnp.concatenate([coupling.reshape(-1, points), stiffness], axis=0)
    thi, tlo = tables(flag, elem_base, elem_nbr[0], ops, points)
    u, edges = first_step(flag, xt, left, right, thi, tlo, elem_metric[0], atm_vertical)
    flux, sent, edge_down, edge_up = fluxes(
        flag,
        pair_owner[0, :, 0],
        pair_block[0],
        pair_src[0],
        tops,
        remap_weight[0],
        bulk_coef[0],
        state[:, levels - 1],
        edges,
        ocean_blocks,
    )
    left2 = lax.ppermute(edge_up, both, atm_up)
    right2 = lax.ppermute(edge_down, both, [(j, i) for i, j in atm_up])

    ocean_new = ocean_step(
        flag, cell_base, ocean, left, right, cell_nbr[0], cell_diff[0], ocean_vertical, sea_mask
    )

    by_owner = lax.all_to_all(
        sent.reshape(n_dom, ocean_blocks, fields, BLK), "dom", split_axis=0, concat_axis=0, tiled=True
    )
    mine = jnp.sum(by_owner, axis=0)
    arrived = jnp.stack([lax.ppermute(mine, both, to_ocean(c)) for c in range(live)])

    atm_next = second_step(flag, u, left2, right2, thi, tlo, elem_metric[0], atm_vertical, flux)
    ocean_next = finish(flag, ocean_new, arrived, sea_mask)
    return (atm_next.reshape(state.shape)[None], ocean_next[None])


def solution(mesh):
    in_specs = (
        P("comp", None, None, None, "dom"),
        P("comp", None, "dom"),
        P("comp", None, "dom"),
        P("comp", None, "dom"),
        P(),
        P(),
        P(),
        P("comp", None, None, "dom"),
        P("comp", None, "dom"),
        P("comp", None, "dom"),
        P(),
        P("comp", "dom"),
        P("comp", "dom", None),
        P("comp", "dom"),
        P("comp", "dom"),
        P("comp", "dom", None, None),
    )
    out_specs = (P("comp", None, None, None, "dom"), P("comp", None, None, "dom"))
    return jax.shard_map(local, mesh=mesh, in_specs=in_specs, out_specs=out_specs, check_vma=False)
```

```python
import functools

import jax
import jax.numpy as jnp
from jax import lax
from jax.experimental import pallas as pl
from jax.experimental.pallas import tpu as pltpu
from jax.sharding import PartitionSpec as P

RIM = 8
BLK = 128
HALO_O = 128
LANES = 128
GROUP = 8

F32 = jnp.float32
BF16 = jnp.bfloat16
ANY = pl.BlockSpec(memory_space=pl.ANY)
HBM = pl.BlockSpec(memory_space=pltpu.HBM)
SMEM = pl.BlockSpec(memory_space=pltpu.SMEM)
VMEM = pl.BlockSpec(memory_space=pltpu.VMEM)


def params(mib):
    return pltpu.CompilerParams(vmem_limit_bytes=mib << 20)


def cost(flops, moved):
    return pl.CostEstimate(flops=flops, bytes_accessed=moved, transcendentals=0)


def split(x):
    hi = x.astype(BF16)
    return hi, (x - hi.astype(F32)).astype(BF16)


def dot(a, b):
    return jnp.dot(a, b, preferred_element_type=F32)


def dot_t(a, b):
    return lax.dot_general(a, b, (((1,), (1,)), ((), ())), preferred_element_type=F32)


def turned(rows):
    n = rows.shape[0]
    if n < LANES:
        rows = jnp.concatenate([rows, jnp.zeros((LANES - n, LANES), rows.dtype)], axis=0)
    return rows.T


OCEAN, DOM, ELEM, CELL = range(4)


def copies(pairs, sem):
    return [pltpu.make_async_copy(a, b, sem.at[i]) for i, (a, b) in enumerate(pairs)]


def start(many):
    for one in many:
        one.start()


def wait(many):
    for one in many:
        one.wait()


def hand_out(dom, low_high, to_core, to_chip):
    core = dom[0] % 2
    to_core[...] = low_high[1 - core]
    to_chip[...] = low_high[core]


def take_in(dom, from_core, from_chip, f):
    first = dom[0] % 2 == 0
    a, b = from_core[f], from_chip[f]
    return jnp.where(first, b, a), jnp.where(first, a, b)


def turn_kernel(ocean, dom, x, o, xt, to_core, to_chip, surface, xv, tv, hv, in_sem, out_sem, o_sem):
    fields, points = xv.shape[0], 16
    olev, cells = o.shape[1], o.shape[2]
    groups = LANES // GROUP

    @pl.when(ocean[0] == 0)
    def _():
        loads = copies([(x.at[f], xv.at[f]) for f in range(fields)], in_sem)
        start(loads)
        outs = []
        levels = xv.shape[1] // points
        for f in range(fields):
            loads[f].wait()
            surface[f] = xv[f, pl.ds((levels - 1) * points, points), :]
            hi_at, lo_at = pl.ds(f * LANES, LANES), pl.ds((fields + f) * LANES, LANES)
            for q in range(0, points, 2):
                one = xv[f, pl.ds(q, LANES, stride=points), :].T
                two = xv[f, pl.ds(q + 1, LANES, stride=points), :].T
                for g in range(groups):
                    part = slice(g * GROUP, (g + 1) * GROUP)
                    rows = jnp.concatenate([one[part], two[part]], axis=0)
                    if g == 0:
                        hv[0, f, pl.ds(q * GROUP, 2 * GROUP), :] = rows
                    if g == groups - 1:
                        hv[1, f, pl.ds(q * GROUP, 2 * GROUP), :] = rows
                    hi, lo = split(rows)
                    at = pl.ds((g * points + q) * GROUP, 2 * GROUP)
                    tv[at, hi_at] = hi
                    tv[at, lo_at] = lo
            outs += copies([(tv.at[:, at], xt.at[:, at]) for at in (hi_at, lo_at)], out_sem.at[f])
            start(outs[-2:])
        hand_out(dom, hv, to_core, to_chip)
        wait(outs)

    @pl.when(ocean[0] != 0)
    def _():
        pairs = []
        for f in range(fields):
            pairs.append((o.at[f, :, pl.ds(0, HALO_O)], hv.at[0, f, pl.ds(0, olev)]))
            pairs.append((o.at[f, :, pl.ds(cells - HALO_O, HALO_O)], hv.at[1, f, pl.ds(0, olev)]))
        loads = copies(pairs, o_sem)
        start(loads)
        wait(loads)
        hand_out(dom, hv, to_core, to_chip)


def turn(ocean_flag, dom, state, ocean):
    fields, levels, points, elems = state.shape
    rows = points * elems
    halo = jax.ShapeDtypeStruct((fields, LANES, LANES), F32)
    return pl.pallas_call(
        turn_kernel,
        out_shape=(
            jax.ShapeDtypeStruct((rows, 2 * fields * LANES), BF16),
            halo,
            halo,
            jax.ShapeDtypeStruct((fields, points, elems), F32),
        ),
        in_specs=[SMEM, SMEM, ANY, ANY],
        out_specs=(ANY, VMEM, VMEM, VMEM),
        scratch_shapes=[
            pltpu.VMEM((fields, levels * points, elems), F32),
            pltpu.VMEM((rows, 2 * fields * LANES), BF16),
            pltpu.VMEM((2, fields, LANES, LANES), F32),
            pltpu.SemaphoreType.DMA((fields,)),
            pltpu.SemaphoreType.DMA((fields, 2)),
            pltpu.SemaphoreType.DMA((2 * fields,)),
        ],
        compiler_params=params(60),
        cost_estimate=cost(2_000_000_000, 9 << 20),
        name="turn_state",
    )(ocean_flag, dom, state.reshape(fields, levels * points, elems), ocean)


def table_kernel(ocean, base, nbr, coupling, stiffness, out, cx, nt, table, sem):
    blocks = table.shape[0]
    points = stiffness.shape[0]
    sides = nbr.shape[0]

    @pl.when(ocean[0] == 0)
    def _():
        nt[...] = turned((nbr[...] - base[0]).astype(F32))
        spread = lax.broadcasted_iota(jnp.int32, (points, LANES), 1) // GROUP
        spread = (spread == lax.broadcasted_iota(jnp.int32, (points, LANES), 0)).astype(F32)
        for ops, first in ((coupling, 0), (stiffness, sides * points)):
            cx[pl.ds(first, ops.shape[0]), :] = jnp.dot(
                ops[...], spread, precision=lax.Precision.HIGHEST, preferred_element_type=F32
            )
        lane = lax.broadcasted_iota(jnp.int32, (GROUP, LANES), 1) % GROUP
        lane_f = lane.astype(F32)
        same = lane == lax.broadcasted_iota(jnp.int32, (GROUP, LANES), 0)
        zero = jnp.zeros((LANES, LANES), BF16)

        @pl.loop(0, blocks)
        def _(block):
            for g in range(2):
                first = pl.multiple_of(block * 2 * GROUP + g * GROUP, GROUP)
                own = nt[pl.ds(first, GROUP), :]
                cols = [jnp.broadcast_to(own[:, s : s + 1], (GROUP, LANES)) for s in range(sides)]
                masks = {}
                for h in range(4):
                    if h - g not in (0, 1, 2):
                        at = pl.ds(h * LANES, LANES)
                        table[block, pl.ds(g * LANES, LANES), at] = zero
                        table[block, pl.ds((2 + g) * LANES, LANES), at] = zero
                        continue
                    begin = (block * 2 * GROUP + (h - 1) * GROUP).astype(F32)
                    masks[h] = [col - begin == lane_f for col in cols]
                for p in range(0, points, 2):
                    rows = [
                        [
                            jnp.broadcast_to(cx[pl.ds(s * points + pp, 1), :], (GROUP, LANES))
                            for s in range(sides + 1)
                        ]
                        for pp in (p, p + 1)
                    ]
                    for h in masks:
                        pair = []
                        for row in rows:
                            total = jnp.where(masks[h][0], row[0], 0.0)
                            for s in range(1, sides):
                                total = total + jnp.where(masks[h][s], row[s], 0.0)
                            if h == g + 1:
                                total = total + jnp.where(same, row[sides], 0.0)
                            pair.append(total)
                        top, rest = split(jnp.concatenate(pair, axis=0))
                        at = pl.ds(h * LANES, LANES)
                        table[block, pl.ds(g * LANES + p * GROUP, 2 * GROUP), at] = top
                        table[block, pl.ds((2 + g) * LANES + p * GROUP, 2 * GROUP), at] = rest
            pltpu.make_async_copy(table.at[block], out.at[block], sem.at[block]).start()

        wait(copies([(table.at[b], out.at[b]) for b in range(blocks)], sem))


def tables(ocean_flag, base, nbr, coupling, stiffness):
    points = stiffness.shape[0]
    sides = nbr.shape[0]
    blocks = nbr.shape[1] // (2 * GROUP)
    return pl.pallas_call(
        table_kernel,
        out_shape=jax.ShapeDtypeStruct((blocks, 4 * LANES, 4 * LANES), BF16),
        in_specs=[SMEM, SMEM, VMEM, VMEM, VMEM],
        out_specs=ANY,
        scratch_shapes=[
            pltpu.VMEM(((sides + 1) * points, LANES), F32),
            pltpu.VMEM((LANES, LANES), F32),
            pltpu.VMEM((blocks, 4 * LANES, 4 * LANES), BF16),
            pltpu.SemaphoreType.DMA((blocks,)),
        ],
        compiler_params=params(58),
        cost_estimate=cost(4_000_000_000, 4 << 20),
        name="neighbour_tables",
    )(ocean_flag, base, nbr, coupling.reshape(sides * points, points), stiffness)


def put_split(xhl, at, f, fields, x):
    hi, lo = split(x)
    xhl[at, pl.ds(f * LANES, LANES)] = hi
    xhl[at, pl.ds((fields + f) * LANES, LANES)] = lo


def columns(turned_rows, first, points):
    pieces = []
    for g in range(2):
        own = turned_rows[pl.ds(pl.multiple_of(first + g * GROUP, GROUP), GROUP), :]
        pieces += [jnp.broadcast_to(own[:, q : q + 1], (GROUP, LANES)) for q in range(points)]
    return jnp.concatenate(pieces, axis=0)


def advance(window, table, wa, mt, element, points, store):
    fields = window.shape[1] // (2 * LANES)
    width = fields * LANES
    rows = 2 * LANES
    heads = dot(table[...], window[:, pl.ds(0, width)])
    rest = dot(table[pl.ds(0, rows), :], window[:, pl.ds(width, width)])
    inner = pl.ds(LANES, rows)
    hi = [window[inner, f * LANES : (f + 1) * LANES] for f in range(fields)]
    lo = [window[inner, (fields + f) * LANES : (fields + f + 1) * LANES] for f in range(fields)]
    v = dot(jnp.concatenate([jnp.concatenate([a, b], axis=1) for a, b in zip(hi, lo)], axis=0), wa[...])
    m = columns(mt, element, points)
    for f in range(fields):
        at = slice(f * LANES, (f + 1) * LANES)
        own = slice(f * rows, (f + 1) * rows)
        tend = heads[:rows, at] + heads[rows:, at] + rest[:, at] + v[own, :LANES] + v[own, LANES:]
        store(f, hi[f].astype(F32) + lo[f].astype(F32) + m * tend)


def prepare(metric, vertical, wa, mt):
    mt[...] = turned(metric[...])
    hi, lo = split(vertical[...].T)
    wa[pl.ds(0, LANES), pl.ds(0, LANES)] = hi
    wa[pl.ds(LANES, LANES), pl.ds(0, LANES)] = hi
    wa[pl.ds(0, LANES), pl.ds(LANES, LANES)] = lo
    wa[pl.ds(LANES, LANES), pl.ds(LANES, LANES)] = jnp.zeros((LANES, LANES), BF16)


def put_flux(ft, flux):
    for f in range(flux.shape[0]):
        ft[f] = turned(-0.5 * flux[f])


def edge_windows(dom, xhl, x, from_core, from_chip):
    fields = from_core.shape[0]
    rows = x.shape[0]
    side = 3 * LANES
    xhl[pl.ds(LANES, side), :] = x[pl.ds(0, side), :]
    xhl[pl.ds(4 * LANES, side), :] = x[pl.ds(rows - side, side), :]
    for f in range(fields):
        left, right = take_in(dom, from_core, from_chip, f)
        put_split(xhl, pl.ds(0, LANES), f, fields, left)
        put_split(xhl, pl.ds(7 * LANES, LANES), f, fields, right)


def edge_kernel(ocean, dom, xt, from_core, from_chip, table, metric, vertical, flux, u, to_core, to_chip, xhl, hv, wa, mt, ft):
    fields, points = flux.shape[0], flux.shape[1]
    blocks = table.shape[0]

    @pl.when(ocean[0] == 0)
    def _():
        prepare(metric, vertical, wa, mt)
        put_flux(ft, flux)
        edge_windows(dom, xhl, xt, from_core, from_chip)
        last_lane = lax.broadcasted_iota(jnp.int32, (2 * LANES, LANES), 1) == LANES - 1
        for i in range(2):
            b = i * (blocks - 1)
            element = b * 2 * GROUP

            def store(f, value):
                value = value + jnp.where(last_lane, columns(ft.at[f], element, points), 0.0)
                put_split(u, pl.ds(i * 2 * LANES, 2 * LANES), f, fields, value)
                hv[i, f] = value[:LANES] if i == 0 else value[LANES:]

            advance(xhl.at[pl.ds(i * 4 * LANES, 4 * LANES)], table.at[b], wa, mt, element, points, store)
        hand_out(dom, hv, to_core, to_chip)


def edge_step(ocean_flag, dom, xt, from_core, from_chip, table, metric, vertical, flux):
    width = xt.shape[1]
    fields = flux.shape[0]
    halo = jax.ShapeDtypeStruct((fields, LANES, LANES), F32)
    return pl.pallas_call(
        edge_kernel,
        out_shape=(jax.ShapeDtypeStruct((4 * LANES, width), BF16), halo, halo),
        in_specs=[SMEM, SMEM] + [VMEM] * 7,
        out_specs=(VMEM, VMEM, VMEM),
        scratch_shapes=[
            pltpu.VMEM((8 * LANES, width), BF16),
            pltpu.VMEM((2, fields, LANES, LANES), F32),
            pltpu.VMEM((2 * LANES, 2 * LANES), BF16),
            pltpu.VMEM((LANES, LANES), F32),
            pltpu.VMEM((fields, LANES, LANES), F32),
        ],
        compiler_params=params(12),
        cost_estimate=cost(4_000_000_000, 3 << 20),
        name="edge_step",
    )(ocean_flag, dom, xt, from_core, from_chip, table, metric, vertical, flux)


def inner_kernel(
    ocean, dom, base, xt, ue, table, metric, vertical, flux, o, from_core, from_chip, nbr, diff, sea, overt,
    u, fresh, zeroed,
    wa, mt, ft, ov, ext, res, zv, o_sem, z_sem, r_sem,
):
    fields, points = flux.shape[0], flux.shape[1]
    rows = xt.shape[0]
    blocks = table.shape[0]
    edge = 2 * LANES

    @pl.when(ocean[0] == 0)
    def _():
        res[0] = jnp.zeros_like(res[0])
        zeros = copies([(res.at[0], fresh.at[f]) for f in range(fields)], z_sem)
        start(zeros)
        prepare(metric, vertical, wa, mt)
        put_flux(ft, flux)
        u[pl.ds(0, edge), :] = ue[pl.ds(0, edge), :]
        u[pl.ds(rows - edge, edge), :] = ue[pl.ds(edge, edge), :]
        last_lane = lax.broadcasted_iota(jnp.int32, (edge, LANES), 1) == LANES - 1

        @pl.loop(1, blocks - 1)
        def _(b):
            first = pl.multiple_of(b * edge, edge)
            element = b * 2 * GROUP

            def store(f, value):
                value = value + jnp.where(last_lane, columns(ft.at[f], element, points), 0.0)
                put_split(u, pl.ds(first, edge), f, fields, value)

            window = xt.at[pl.ds(pl.multiple_of(first - LANES, LANES), 4 * LANES)]
            advance(window, table.at[b], wa, mt, element, points, store)

        wait(zeros)

    @pl.when(ocean[0] != 0)
    def _():
        load = pltpu.make_async_copy(o, ov, o_sem.at[0])
        load.start()
        zv[...] = jnp.zeros_like(zv)
        zeros = copies([(zv, zeroed.at[f]) for f in range(fields)], z_sem)
        start(zeros)
        ocean_part(dom, base, load, from_core, from_chip, nbr, diff, sea, overt, fresh, ov, ext, res, r_sem)
        wait(zeros)


def ocean_part(dom, base, load, from_core, from_chip, nbr, diff, sea, overt, fresh, ov, ext, res, r_sem):
    fields, olev, cells = ov.shape
    sides = nbr.shape[0]
    for f in range(fields):
        rows = pl.ds(f * olev, olev)
        left, right = take_in(dom, from_core, from_chip, f)
        for at, value in ((0, left[:olev]), (HALO_O + cells, right[:olev])):
            hi, lo = split(value)
            ext[0, rows, pl.ds(at, HALO_O)] = hi
            ext[1, rows, pl.ds(at, HALO_O)] = lo
    load.wait()
    for f in range(fields):
        rows = pl.ds(f * olev, olev)
        hi, lo = split(ov[f])
        ext[0, rows, pl.ds(HALO_O, cells)] = hi
        ext[1, rows, pl.ds(HALO_O, cells)] = lo
    vhi, vlo = split(overt[...])

    @pl.loop(0, cells // LANES)
    def _(b):
        first = pl.multiple_of(b * LANES, LANES)
        here = pl.ds(first, LANES)
        begin = base[0] + first - HALO_O
        place = lax.broadcasted_iota(jnp.int32, (3 * LANES, LANES), 0)
        table = jnp.zeros((3 * LANES, LANES), F32)
        held = jnp.zeros((1, LANES), F32)
        for k in range(sides):
            d = diff[k, :, here]
            held = held + d
            table = table + jnp.where(place == nbr[k, :, here] - begin, d, 0.0)
        hi, lo = split(table)
        window = pl.ds(first, 3 * LANES)
        lap = dot(ext[0, :, window], hi) + dot(ext[1, :, window], hi) + dot(ext[0, :, window], lo)
        inner = pl.ds(pl.multiple_of(first + HALO_O, LANES), LANES)
        wet = sea[:, here] == 1
        for f in range(fields):
            rows = pl.ds(f * olev, olev)
            xhi, xlo = ext[0, rows, inner], ext[1, rows, inner]
            v = dot(vhi, xhi) + dot(vhi, xlo) + dot(vlo, xhi)
            own = ov[f, :, here]
            new = own + (lap[f * olev : (f + 1) * olev] - held * own) + v
            res[f, :, here] = jnp.where(wet, new, own)

    out = pltpu.make_async_copy(res, fresh, r_sem.at[0])
    out.start()
    out.wait()


def inner_step(
    ocean_flag, dom, base, xt, ue, table, metric, vertical, flux, ocean, from_core, from_chip, nbr, diff, sea, overt
):
    rows, width = xt.shape
    fields, points = flux.shape[0], flux.shape[1]
    olev, cells = ocean.shape[1], ocean.shape[2]
    return pl.pallas_call(
        inner_kernel,
        out_shape=(
            jax.ShapeDtypeStruct((rows, width), BF16),
            jax.ShapeDtypeStruct(ocean.shape, F32),
            jax.ShapeDtypeStruct((fields, rows, LANES), F32),
        ),
        in_specs=[SMEM, SMEM, SMEM] + [VMEM] * 6 + [HBM] + [VMEM] * 6,
        out_specs=(VMEM, HBM, HBM),
        scratch_shapes=[
            pltpu.VMEM((2 * LANES, 2 * LANES), BF16),
            pltpu.VMEM((LANES, LANES), F32),
            pltpu.VMEM((fields, LANES, LANES), F32),
            pltpu.VMEM(ocean.shape, F32),
            pltpu.VMEM((2, fields * olev, cells + 2 * HALO_O), BF16),
            pltpu.VMEM(ocean.shape, F32),
            pltpu.VMEM((rows, LANES), F32),
            pltpu.SemaphoreType.DMA((1,)),
            pltpu.SemaphoreType.DMA((fields,)),
            pltpu.SemaphoreType.DMA((1,)),
        ],
        compiler_params=params(20),
        cost_estimate=cost(10_000_000_000, 10 << 20),
        name="inner_step",
    )(ocean_flag, dom, base, xt, ue, table, metric, vertical, flux, ocean, from_core, from_chip, nbr, diff, sea, overt)


def flux_kernel(ocean, dom, owner, block, source, *refs):
    n_tops = len(refs) - 9
    tops = refs[:n_tops]
    weights, coef, sv, flux, sent, tv, wcat, surf, fl = refs[n_tops:]
    pairs = weights.shape[0]
    points, fields = coef.shape[0], flux.shape[0]
    ocean_blocks = sent.shape[0] // n_tops
    chips = n_tops // 2

    @pl.when(ocean[0] == 0)
    def _():
        surf[...] = jnp.zeros_like(surf)
        sent[...] = jnp.zeros_like(sent)
        chip, core = dom[0] // 2, dom[0] % 2

        def doubled(rows):
            hi, lo = split(rows)
            eight = jnp.concatenate([hi.astype(F32), lo.astype(F32)], axis=0).astype(BF16)
            return jnp.concatenate([eight, eight], axis=1)

        @pl.loop(0, pairs, unroll=4)
        def _(r):
            hi, lo = split(weights[r])
            wcat[r, :, pl.ds(0, BLK)] = hi
            wcat[r, :, pl.ds(BLK, BLK)] = lo

        for i in range(n_tops):
            tv[i] = tops[i][...]
        for r in range(pairs):
            at = pl.multiple_of(block[r] * BLK, BLK)
            which = owner[r]
            slot = ((which // 2) ^ chip) + jnp.where(which % 2 == core, 0, chips)
            rows = doubled(tv[slot, :, pl.ds(at, BLK)])
            out = dot_t(rows, wcat[r])
            surf[source[r]] += out[:fields] + out[fields:]

        for p in range(points):
            value = coef[pl.ds(p, 1), :] * (sv[:, p, :] - surf[p])
            fl[p] = value
            flux[:, p, :] = value

        for r in range(pairs):
            rows = doubled(fl[source[r]])
            both = jnp.concatenate([wcat[r, :, pl.ds(0, BLK)], wcat[r, :, pl.ds(BLK, BLK)]], axis=0)
            out = dot(rows, both)
            sent[owner[r] * ocean_blocks + block[r]] += out[:fields] + out[fields:]


def fluxes(ocean_flag, dom, owner, block, source, tops, weights, coef, surface, ocean_blocks):
    fields, points, elems = surface.shape
    pairs = weights.shape[0]
    n = len(tops)
    return pl.pallas_call(
        flux_kernel,
        out_shape=(
            jax.ShapeDtypeStruct((fields, points, elems), F32),
            jax.ShapeDtypeStruct((n * ocean_blocks, fields, BLK), F32),
        ),
        in_specs=[SMEM] * 5 + [VMEM] * (n + 3),
        out_specs=(VMEM, VMEM),
        scratch_shapes=[
            pltpu.VMEM((n,) + tops[0].shape, F32),
            pltpu.VMEM((pairs, BLK, 2 * BLK), BF16),
            pltpu.VMEM((points, fields, BLK), F32),
            pltpu.VMEM((points, fields, BLK), F32),
        ],
        compiler_params=params(8),
        cost_estimate=cost(4_000_000_000, 4 << 20),
        name="fluxes",
    )(ocean_flag, dom, owner, block, source, *tops, weights, coef, surface)


def second_kernel(ocean, dom, u, from_core, from_chip, table, metric, vertical, flux, held, out, xhl, wa, mt, xv, ov, o_sem):
    del held
    fields, points = flux.shape[0], flux.shape[1]
    rows, levels = xv.shape[1], xv.shape[2]
    blocks = table.shape[0]
    edge = 2 * LANES

    @pl.when(ocean[0] == 0)
    def _():
        prepare(metric, vertical, wa, mt)
        edge_windows(dom, xhl, u, from_core, from_chip)

        def step(b, window):
            def store(f, value):
                xv[f, pl.ds(b * edge if isinstance(b, int) else pl.multiple_of(b * edge, edge), edge), :] = value

            advance(window, table.at[b], wa, mt, b * 2 * GROUP, points, store)

        @pl.loop(1, blocks - 1)
        def _(b):
            step(b, u.at[pl.ds(pl.multiple_of(b * edge - LANES, LANES), 4 * LANES)])

        step(0, xhl.at[pl.ds(0, 4 * LANES)])
        step(blocks - 1, xhl.at[pl.ds(4 * LANES, 4 * LANES)])
        outs = copies([(ov.at[f], out.at[f]) for f in range(fields)], o_sem)
        for f in range(fields):
            for p in range(points):
                cols = [xv[f, pl.ds(g * LANES + p * GROUP, GROUP), :] for g in range(LANES // GROUP)]
                ov[f, pl.ds(p, LANES, stride=points), :] = jnp.concatenate(cols, axis=0).T
            last = pl.ds((levels - 1) * points, points)
            ov[f, last, :] = ov[f, last, :] - 0.5 * flux[f]
            outs[f].start()
        wait(outs)


def second_step(ocean_flag, dom, u, from_core, from_chip, table, metric, vertical, flux, zeroed, levels):
    fields, points = flux.shape[0], flux.shape[1]
    rows, width = u.shape
    return pl.pallas_call(
        second_kernel,
        out_shape=jax.ShapeDtypeStruct((fields, levels * points, LANES), F32),
        in_specs=[SMEM, SMEM] + [VMEM] * 7 + [HBM],
        out_specs=HBM,
        input_output_aliases={9: 0},
        scratch_shapes=[
            pltpu.VMEM((8 * LANES, width), BF16),
            pltpu.VMEM((2 * LANES, 2 * LANES), BF16),
            pltpu.VMEM((LANES, LANES), F32),
            pltpu.VMEM((fields, rows, levels), F32),
            pltpu.VMEM((fields, levels * points, LANES), F32),
            pltpu.SemaphoreType.DMA((fields,)),
        ],
        compiler_params=params(20),
        cost_estimate=cost(10_000_000_000, 12 << 20),
        name="second_step",
    )(ocean_flag, dom, u, from_core, from_chip, table, metric, vertical, flux, zeroed)


def gather_kernel(ocean, dom, a, b, c, same, other):
    chips = same.shape[0]
    per = same.shape[1]

    @pl.when(ocean[0] != 0)
    def _():
        chip, core = dom[0] // 2, dom[0] % 2
        for out, side in ((same, 0), (other, 1)):
            for s in range(chips):
                at = pl.ds(((chip ^ s) * 2 + (core ^ side)) * per, per)
                out[s] = a[at] + b[at] + c[at]


def gather_sent(ocean_flag, dom, parts, chips):
    total, fields, blk = parts[0].shape
    per = total // (2 * chips)
    shape = jax.ShapeDtypeStruct((chips, per, fields, blk), F32)
    return pl.pallas_call(
        gather_kernel,
        out_shape=(shape, shape),
        in_specs=[SMEM, SMEM, VMEM, VMEM, VMEM],
        out_specs=(VMEM, VMEM),
        compiler_params=params(4),
        cost_estimate=cost(0, 1 << 19),
        name="gather_sent",
    )(ocean_flag, dom, *parts)


def pair_kernel(ocean, same, other, *outs):
    @pl.when(ocean[0] != 0)
    def _():
        for s, out in enumerate(outs):
            out[...] = same[s] + other[s]


def pair_sums(ocean_flag, same, other):
    chips = same.shape[0]
    return pl.pallas_call(
        pair_kernel,
        out_shape=(jax.ShapeDtypeStruct(same.shape[1:], F32),) * chips,
        in_specs=[SMEM, VMEM, VMEM],
        out_specs=(VMEM,) * chips,
        compiler_params=params(4),
        cost_estimate=cost(0, 1 << 18),
        name="pair_sums",
    )(ocean_flag, same, other)


def finish_kernel(ocean, fresh, sea, *refs):
    del fresh
    n = len(refs) - 4
    parts, (out, rows_v, in_sem, out_sem) = refs[:n], refs[n:]
    fields, cells = rows_v.shape[0], rows_v.shape[2]

    @pl.when(ocean[0] != 0)
    def _():
        loads = copies([(out.at[f, pl.ds(0, 8)], rows_v.at[f]) for f in range(fields)], in_sem)
        start(loads)
        wait(loads)
        for b in range(cells // BLK):
            here = pl.ds(b * BLK, BLK)
            total = parts[0][b]
            for part in parts[1:]:
                total = total + part[b]
            total = jnp.where(sea[:, here] == 1, 0.5 * total, 0.0)
            for f in range(fields):
                rows_v[f, pl.ds(0, 1), here] = rows_v[f, pl.ds(0, 1), here] + total[f : f + 1]
        stores = copies([(rows_v.at[f], out.at[f, pl.ds(0, 8)]) for f in range(fields)], out_sem)
        start(stores)
        wait(stores)


def finish(ocean_flag, fresh, parts, sea):
    fields, olev, cells = fresh.shape
    return pl.pallas_call(
        finish_kernel,
        out_shape=jax.ShapeDtypeStruct(fresh.shape, F32),
        in_specs=[SMEM, HBM] + [VMEM] * (1 + len(parts)),
        out_specs=HBM,
        input_output_aliases={1: 0},
        scratch_shapes=[
            pltpu.VMEM((fields, 8, cells), F32),
            pltpu.SemaphoreType.DMA((fields,)),
            pltpu.SemaphoreType.DMA((fields,)),
        ],
        compiler_params=params(4),
        cost_estimate=cost(0, 1 << 18),
        name="finish_ocean",
    )(ocean_flag, fresh, sea, *parts)


def local(
    atm_state,
    elem_nbr,
    elem_metric,
    bulk_coef,
    stiffness,
    coupling,
    atm_vertical,
    ocean_state,
    cell_nbr,
    cell_diff,
    ocean_vertical,
    sea_mask,
    pair_owner,
    pair_block,
    pair_src,
    remap_weight,
):
    n_comp = lax.axis_size("comp")
    n_dom = lax.axis_size("dom")
    comp_index = lax.axis_index("comp")
    dom_index = lax.axis_index("dom")
    live = n_comp - 1
    chips = n_dom // 2
    state = atm_state[0]
    ocean = ocean_state[0]
    fields, levels, points, elems = state.shape
    cells = ocean.shape[2]
    ocean_blocks = cells // BLK
    one = lambda value: value.astype(jnp.int32).reshape(1)
    flag = one(comp_index == live)
    dom = one(dom_index)
    elem_base = one((comp_index * n_dom + dom_index) * elems)
    cell_base = one(dom_index * cells)

    both = ("comp", "dom")
    swapped = [(d, d ^ 1) for d in range(n_dom)]
    between = [(i, i + 1) for i in range(1, live * n_dom - 1, 2)]
    atm_chips = between + [(j, i) for i, j in between]
    between = [(live * n_dom + i, live * n_dom + i + 1) for i in range(1, n_dom - 1, 2)]
    all_chips = atm_chips + between + [(j, i) for i, j in between]

    def from_ocean(c):
        return [(live * n_dom + d, c * n_dom + d) for d in range(n_dom)]

    def to_ocean(c):
        return [(j, i) for i, j in from_ocean(c)]

    def shifted(by):
        return [(d, d ^ (2 * by)) for d in range(n_dom)]

    def among_ocean(pairs):
        return [(live * n_dom + a, live * n_dom + b) for a, b in pairs]

    top = ocean[:, 0, :]
    brought = [lax.ppermute(top, both, from_ocean(c)) for c in range(live)]
    xt, to_core, to_chip, surface = turn(flag, dom, state, ocean)
    brought, to_core, to_chip = lax.optimization_barrier((brought, to_core, to_chip))
    from_core = lax.ppermute(to_core, "dom", swapped)
    from_chip = lax.ppermute(to_chip, both, all_chips)
    got = sum(brought)
    near = [got] + [lax.ppermute(got, "dom", shifted(s)) for s in range(1, chips)]
    nbr, got = lax.optimization_barrier((elem_nbr[0], got))
    table = tables(flag, elem_base, nbr, coupling, stiffness)
    near, table = lax.optimization_barrier((near, table))
    tops = near + [lax.ppermute(part, "dom", swapped) for part in near]

    flux, sent = fluxes(
        flag,
        dom,
        pair_owner[0, :, 0],
        pair_block[0],
        pair_src[0],
        tops,
        remap_weight[0],
        bulk_coef[0],
        surface,
        ocean_blocks,
    )
    parts = [lax.ppermute(sent, both, to_ocean(c)) for c in range(live)]
    metric = elem_metric[0]
    ue, to_core, to_chip = edge_step(flag, dom, xt, from_core, from_chip, table, metric, atm_vertical, flux)
    from_core2 = lax.ppermute(to_core, "dom", swapped)
    from_chip2 = lax.ppermute(to_chip, both, atm_chips)

    u, fresh, zeroed = inner_step(
        flag,
        dom,
        cell_base,
        xt,
        ue,
        table,
        metric,
        atm_vertical,
        flux,
        ocean,
        from_core,
        from_chip,
        cell_nbr[0][:, None],
        cell_diff[0][:, None],
        sea_mask,
        ocean_vertical,
    )

    parts, u = lax.optimization_barrier((parts, u))
    same, other = gather_sent(flag, dom, parts, chips)
    arrived = lax.ppermute(other, both, among_ocean(swapped))
    pieces = pair_sums(flag, same, arrived)
    mine = [pieces[0]] + [
        lax.ppermute(pieces[s], both, among_ocean(shifted(s))) for s in range(1, chips)
    ]

    atm_next = second_step(flag, dom, u, from_core2, from_chip2, table, metric, atm_vertical, flux, zeroed, levels)
    ocean_next = finish(flag, fresh, mine, sea_mask)
    return (atm_next.reshape(state.shape)[None], ocean_next[None])


def solution(mesh):
    in_specs = (
        P("comp", None, None, None, "dom"),
        P("comp", None, "dom"),
        P("comp", None, "dom"),
        P("comp", None, "dom"),
        P(),
        P(),
        P(),
        P("comp", None, None, "dom"),
        P("comp", None, "dom"),
        P("comp", None, "dom"),
        P(),
        P("comp", "dom"),
        P("comp", "dom", None),
        P("comp", "dom"),
        P("comp", "dom"),
        P("comp", "dom", None, None),
    )
    out_specs = (P("comp", None, None, None, "dom"), P("comp", None, None, "dom"))
    return jax.shard_map(local, mesh=mesh, in_specs=in_specs, out_specs=out_specs, check_vma=False)
```

```python
import functools

import jax
import jax.numpy as jnp
from jax import lax
from jax.experimental import pallas as pl
from jax.experimental.pallas import tpu as pltpu
from jax.sharding import PartitionSpec as P

RIM = 8
BLK = 128
HALO_O = 128
LANES = 128
GROUP = 8
TURN = 60

F32 = jnp.float32
BF16 = jnp.bfloat16
ANY = pl.BlockSpec(memory_space=pl.ANY)
HBM = pl.BlockSpec(memory_space=pltpu.HBM)
SMEM = pl.BlockSpec(memory_space=pltpu.SMEM)
VMEM = pl.BlockSpec(memory_space=pltpu.VMEM)


def params(mib):
    return pltpu.CompilerParams(vmem_limit_bytes=mib << 20)


def cost(flops, moved):
    return pl.CostEstimate(flops=flops, bytes_accessed=moved, transcendentals=0)


def split(x):
    hi = x.astype(BF16)
    return hi, (x - hi.astype(F32)).astype(BF16)


def dot(a, b):
    return jnp.dot(a, b, preferred_element_type=F32)


def dot_t(a, b):
    return lax.dot_general(a, b, (((1,), (1,)), ((), ())), preferred_element_type=F32)


def turned(rows):
    n = rows.shape[0]
    if n < LANES:
        rows = jnp.concatenate([rows, jnp.zeros((LANES - n, LANES), rows.dtype)], axis=0)
    return rows.T


OCEAN, DOM, ELEM, CELL = range(4)


def copies(pairs, sem):
    return [pltpu.make_async_copy(a, b, sem.at[i]) for i, (a, b) in enumerate(pairs)]


def start(many):
    for one in many:
        one.start()


def wait(many):
    for one in many:
        one.wait()


def hand_out(dom, low_high, to_core, to_chip):
    core = dom[0] % 2
    to_core[...] = low_high[1 - core]
    to_chip[...] = low_high[core]


def take_in(dom, from_core, from_chip, f):
    first = dom[0] % 2 == 0
    a, b = from_core[f], from_chip[f]
    return jnp.where(first, b, a), jnp.where(first, a, b)


def turn_kernel(ocean, dom, x, o, xt, to_core, to_chip, surface, zeroed, xv, tv, hv, in_sem, out_sem, o_sem, z_sem):
    fields, points = xv.shape[0], 16
    olev, cells = o.shape[1], o.shape[2]
    groups = LANES // GROUP

    @pl.when(ocean[0] == 0)
    def _():
        loads = copies([(x.at[f], xv.at[f]) for f in range(fields)], in_sem)
        start(loads)
        outs = []
        levels = xv.shape[1] // points
        for f in range(fields):
            loads[f].wait()
            surface[f] = xv[f, pl.ds((levels - 1) * points, points), :]
            hi_at, lo_at = pl.ds(f * LANES, LANES), pl.ds((fields + f) * LANES, LANES)
            for q in range(0, points, 2):
                one = xv[f, pl.ds(q, LANES, stride=points), :].T
                two = xv[f, pl.ds(q + 1, LANES, stride=points), :].T
                for g in range(groups):
                    part = slice(g * GROUP, (g + 1) * GROUP)
                    rows = jnp.concatenate([one[part], two[part]], axis=0)
                    if g == 0:
                        hv[0, f, pl.ds(q * GROUP, 2 * GROUP), :] = rows
                    if g == groups - 1:
                        hv[1, f, pl.ds(q * GROUP, 2 * GROUP), :] = rows
                    hi, lo = split(rows)
                    at = pl.ds((g * points + q) * GROUP, 2 * GROUP)
                    tv[at, hi_at] = hi
                    tv[at, lo_at] = lo
            outs += copies([(tv.at[:, at], xt.at[:, at]) for at in (hi_at, lo_at)], out_sem.at[f])
            start(outs[-2:])
        hand_out(dom, hv, to_core, to_chip)
        wait(outs)

    @pl.when(ocean[0] != 0)
    def _():
        xv[0] = jnp.zeros_like(xv[0])
        zeros = copies([(xv.at[0], zeroed.at[f]) for f in range(fields)], z_sem)
        pairs = []
        for f in range(fields):
            pairs.append((o.at[f, :, pl.ds(0, HALO_O)], hv.at[0, f, pl.ds(0, olev)]))
            pairs.append((o.at[f, :, pl.ds(cells - HALO_O, HALO_O)], hv.at[1, f, pl.ds(0, olev)]))
        loads = copies(pairs, o_sem)
        start(loads)
        start(zeros)
        wait(loads)
        hand_out(dom, hv, to_core, to_chip)
        wait(zeros)


def turn(ocean_flag, dom, state, ocean):
    fields, levels, points, elems = state.shape
    rows = points * elems
    halo = jax.ShapeDtypeStruct((fields, LANES, LANES), F32)
    return pl.pallas_call(
        turn_kernel,
        out_shape=(
            jax.ShapeDtypeStruct((rows, 2 * fields * LANES), BF16),
            halo,
            halo,
            jax.ShapeDtypeStruct((fields, points, elems), F32),
            jax.ShapeDtypeStruct((fields, levels * points, elems), F32),
        ),
        in_specs=[SMEM, SMEM, ANY, ANY],
        out_specs=(ANY, VMEM, VMEM, VMEM, HBM),
        scratch_shapes=[
            pltpu.VMEM((fields, levels * points, elems), F32),
            pltpu.VMEM((rows, 2 * fields * LANES), BF16),
            pltpu.VMEM((2, fields, LANES, LANES), F32),
            pltpu.SemaphoreType.DMA((fields,)),
            pltpu.SemaphoreType.DMA((fields, 2)),
            pltpu.SemaphoreType.DMA((2 * fields,)),
            pltpu.SemaphoreType.DMA((fields,)),
        ],
        compiler_params=params(TURN),
        cost_estimate=cost(2000000000, 9 << 20),
        name="turn_state",
    )(ocean_flag, dom, state.reshape(fields, levels * points, elems), ocean)


def prepare_table(base, nbr, coupling, stiffness, cx, nt):
    points = stiffness.shape[0]
    nt[...] = turned((nbr[...] - base[0]).astype(F32))
    spread = lax.broadcasted_iota(jnp.int32, (points, LANES), 1) // GROUP
    spread = (spread == lax.broadcasted_iota(jnp.int32, (points, LANES), 0)).astype(F32)
    for ops, first in ((coupling, 0), (stiffness, coupling.shape[0])):
        cx[pl.ds(first, ops.shape[0]), :] = jnp.dot(
            ops[...], spread, precision=lax.Precision.HIGHEST, preferred_element_type=F32
        )


def build_table(block, table, slot, cx, nt, sides, points):
    lane = lax.broadcasted_iota(jnp.int32, (GROUP, LANES), 1) % GROUP
    lane_f = lane.astype(F32)
    same = lane == lax.broadcasted_iota(jnp.int32, (GROUP, LANES), 0)
    zero = jnp.zeros((LANES, LANES), BF16)
    for g in range(2):
        first = pl.multiple_of(block * 2 * GROUP + g * GROUP, GROUP)
        own = nt[pl.ds(first, GROUP), :]
        cols = [jnp.broadcast_to(own[:, s : s + 1], (GROUP, LANES)) for s in range(sides)]
        masks = {}
        for h in range(4):
            if h - g not in (0, 1, 2):
                at = pl.ds(h * LANES, LANES)
                table[slot, pl.ds(g * LANES, LANES), at] = zero
                table[slot, pl.ds((2 + g) * LANES, LANES), at] = zero
                continue
            begin = jnp.asarray(block * 2 * GROUP + (h - 1) * GROUP, jnp.int32).astype(F32)
            masks[h] = [col - begin == lane_f for col in cols]
        for p in range(0, points, 2):
            rows = [
                [jnp.broadcast_to(cx[pl.ds(s * points + pp, 1), :], (GROUP, LANES)) for s in range(sides + 1)]
                for pp in (p, p + 1)
            ]
            for h in masks:
                pair = []
                for row in rows:
                    total = jnp.where(masks[h][0], row[0], 0.0)
                    for s in range(1, sides):
                        total = total + jnp.where(masks[h][s], row[s], 0.0)
                    if h == g + 1:
                        total = total + jnp.where(same, row[sides], 0.0)
                    pair.append(total)
                top, rest = split(jnp.concatenate(pair, axis=0))
                at = pl.ds(h * LANES, LANES)
                table[slot, pl.ds(g * LANES + p * GROUP, 2 * GROUP), at] = top
                table[slot, pl.ds((2 + g) * LANES + p * GROUP, 2 * GROUP), at] = rest


def put_split(xhl, at, f, fields, x):
    hi, lo = split(x)
    xhl[at, pl.ds(f * LANES, LANES)] = hi
    xhl[at, pl.ds((fields + f) * LANES, LANES)] = lo


def columns(turned_rows, first, points):
    pieces = []
    for g in range(2):
        own = turned_rows[pl.ds(pl.multiple_of(first + g * GROUP, GROUP), GROUP), :]
        pieces += [jnp.broadcast_to(own[:, q : q + 1], (GROUP, LANES)) for q in range(points)]
    return jnp.concatenate(pieces, axis=0)


def advance(window, table, wa, mt, element, points, store, chosen):
    fields = window.shape[1] // (2 * LANES)
    rows = 2 * LANES
    n = len(chosen)
    heads = dot(table[...], window[:, pl.ds(chosen[0] * LANES, n * LANES)])
    rest = dot(table[pl.ds(0, rows), :], window[:, pl.ds((fields + chosen[0]) * LANES, n * LANES)])
    inner = pl.ds(LANES, rows)
    hi = [window[inner, f * LANES : (f + 1) * LANES] for f in chosen]
    lo = [window[inner, (fields + f) * LANES : (fields + f + 1) * LANES] for f in chosen]
    v = dot(jnp.concatenate([jnp.concatenate([a, b], axis=1) for a, b in zip(hi, lo)], axis=0), wa[...])
    m = columns(mt, element, points)
    for i, f in enumerate(chosen):
        at = slice(i * LANES, (i + 1) * LANES)
        own = slice(i * rows, (i + 1) * rows)
        tend = heads[:rows, at] + heads[rows:, at] + rest[:, at] + v[own, :LANES] + v[own, LANES:]
        store(f, hi[i].astype(F32) + lo[i].astype(F32) + m * tend)


def prepare(metric, vertical, wa, mt):
    mt[...] = turned(metric[...])
    hi, lo = split(vertical[...].T)
    wa[pl.ds(0, LANES), pl.ds(0, LANES)] = hi
    wa[pl.ds(LANES, LANES), pl.ds(0, LANES)] = hi
    wa[pl.ds(0, LANES), pl.ds(LANES, LANES)] = lo
    wa[pl.ds(LANES, LANES), pl.ds(LANES, LANES)] = jnp.zeros((LANES, LANES), BF16)


def put_flux(ft, flux):
    for f in range(flux.shape[0]):
        ft[f] = turned(-0.5 * flux[f])


def edge_windows(dom, xhl, x, from_core, from_chip):
    fields = from_core.shape[0]
    rows = x.shape[0]
    side = 3 * LANES
    xhl[pl.ds(LANES, side), :] = x[pl.ds(0, side), :]
    xhl[pl.ds(4 * LANES, side), :] = x[pl.ds(rows - side, side), :]
    for f in range(fields):
        left, right = take_in(dom, from_core, from_chip, f)
        put_split(xhl, pl.ds(0, LANES), f, fields, left)
        put_split(xhl, pl.ds(7 * LANES, LANES), f, fields, right)


def edge_kernel(
    ocean, dom, elem, base, xt, from_core, from_chip, enbr, coupling, stiffness, metric, vertical, flux,
    o, nbr, diff, sea, overt, held,
    u, to_core, to_chip, fresh,
    table, cx, nt, xhl, hv, wa, mt, ft, ov, ext, res, vert, o_sem, r_sem,
):
    del held
    fields, points = flux.shape[0], flux.shape[1]
    blocks = xt.shape[0] // (2 * LANES)
    sides = enbr.shape[0]

    @pl.when(ocean[0] == 0)
    def _():
        prepare_table(elem, enbr, coupling, stiffness, cx, nt)
        for i in range(2):
            build_table(i * (blocks - 1), table, i, cx, nt, sides, points)
        prepare(metric, vertical, wa, mt)
        put_flux(ft, flux)
        edge_windows(dom, xhl, xt, from_core, from_chip)
        last_lane = lax.broadcasted_iota(jnp.int32, (2 * LANES, LANES), 1) == LANES - 1
        for i in range(2):
            b = i * (blocks - 1)
            element = b * 2 * GROUP

            def store(f, value):
                value = value + jnp.where(last_lane, columns(ft.at[f], element, points), 0.0)
                put_split(u, pl.ds(i * 2 * LANES, 2 * LANES), f, fields, value)
                hv[i, f] = value[:LANES] if i == 0 else value[LANES:]

            advance(
                xhl.at[pl.ds(i * 4 * LANES, 4 * LANES)], table.at[i], wa, mt, element, points, store, range(fields)
            )
        hand_out(dom, hv, to_core, to_chip)

    @pl.when(ocean[0] != 0)
    def _():
        load = pltpu.make_async_copy(o, ov, o_sem.at[0])
        load.start()
        ocean_part(dom, base, load, from_core, from_chip, nbr, diff, sea, overt, fresh, ov, ext, res, vert, r_sem)


def edge_step(
    ocean_flag, dom, elem, base, xt, from_core, from_chip, enbr, coupling, stiffness, metric, vertical, flux,
    ocean, nbr, diff, sea, overt, fresh,
):
    width = xt.shape[1]
    points = stiffness.shape[0]
    sides = enbr.shape[0]
    fields = flux.shape[0]
    olev, cells = ocean.shape[1], ocean.shape[2]
    halo = jax.ShapeDtypeStruct((fields, LANES, LANES), F32)
    return pl.pallas_call(
        edge_kernel,
        out_shape=(
            jax.ShapeDtypeStruct((4 * LANES, width), BF16),
            halo,
            halo,
            jax.ShapeDtypeStruct(ocean.shape, F32),
        ),
        in_specs=[SMEM] * 4 + [VMEM] * 9 + [HBM] + [VMEM] * 4 + [HBM],
        out_specs=(VMEM, VMEM, VMEM, HBM),
        input_output_aliases={18: 3},
        scratch_shapes=[
            pltpu.VMEM((2, 4 * LANES, 4 * LANES), BF16),
            pltpu.VMEM(((sides + 1) * points, LANES), F32),
            pltpu.VMEM((LANES, LANES), F32),
            pltpu.VMEM((8 * LANES, width), BF16),
            pltpu.VMEM((2, fields, LANES, LANES), F32),
            pltpu.VMEM((2 * LANES, 2 * LANES), BF16),
            pltpu.VMEM((LANES, LANES), F32),
            pltpu.VMEM((fields, LANES, LANES), F32),
            pltpu.VMEM(ocean.shape, F32),
            pltpu.VMEM((2, fields * olev, cells + 2 * HALO_O), BF16),
            pltpu.VMEM(ocean.shape, F32),
            pltpu.VMEM(ocean.shape, F32),
            pltpu.SemaphoreType.DMA((1,)),
            pltpu.SemaphoreType.DMA((1,)),
        ],
        compiler_params=params(20),
        cost_estimate=cost(4000000000, 3 << 20),
        name="edge_step",
    )(
        ocean_flag, dom, elem, base, xt, from_core, from_chip, enbr, coupling, stiffness, metric, vertical, flux,
        ocean, nbr, diff, sea, overt, fresh,
    )


def inner_kernel(ocean, elem, xt, ue, enbr, coupling, stiffness, metric, vertical, flux, u, table, cx, nt, wa, mt, ft):
    fields, points = flux.shape[0], flux.shape[1]
    sides = enbr.shape[0]
    rows = xt.shape[0]
    blocks = table.shape[0]
    edge = 2 * LANES

    @pl.when(ocean[0] == 0)
    def _():
        prepare_table(elem, enbr, coupling, stiffness, cx, nt)
        for b in range(2):
            build_table(b, table, b, cx, nt, sides, points)
        prepare(metric, vertical, wa, mt)
        put_flux(ft, flux)
        u[pl.ds(0, edge), :] = ue[pl.ds(0, edge), :]
        u[pl.ds(rows - edge, edge), :] = ue[pl.ds(edge, edge), :]
        last_lane = lax.broadcasted_iota(jnp.int32, (edge, LANES), 1) == LANES - 1

        @pl.loop(1, blocks - 1, step=3)
        def _(start_of):
            for i in range(3):
                b = start_of + i
                first = pl.multiple_of(b * edge, edge)
                element = b * 2 * GROUP

                def store(f, value):
                    value = value + jnp.where(last_lane, columns(ft.at[f], element, points), 0.0)
                    put_split(u, pl.ds(first, edge), f, fields, value)

                window = xt.at[pl.ds(pl.multiple_of(first - LANES, LANES), 4 * LANES)]
                advance(window, table.at[b], wa, mt, element, points, store, range(fields))
                build_table(b + 1, table, b + 1, cx, nt, sides, points)


def ocean_part(dom, base, load, from_core, from_chip, nbr, diff, sea, overt, fresh, ov, ext, res, vert, r_sem):
    fields, olev, cells = ov.shape
    sides = nbr.shape[0]
    for f in range(fields):
        rows = pl.ds(f * olev, olev)
        left, right = take_in(dom, from_core, from_chip, f)
        for at, value in ((0, left[:olev]), (HALO_O + cells, right[:olev])):
            hi, lo = split(value)
            ext[0, rows, pl.ds(at, HALO_O)] = hi
            ext[1, rows, pl.ds(at, HALO_O)] = lo
    vhi, vlo = split(overt[...])
    both = jnp.concatenate([vhi, vlo], axis=0)
    load.wait()
    for f in range(fields):
        rows = pl.ds(f * olev, olev)
        hi, lo = split(ov[f])
        ext[0, rows, pl.ds(HALO_O, cells)] = hi
        ext[1, rows, pl.ds(HALO_O, cells)] = lo
        v = dot(both, hi)
        vert[f] = v[:olev] + v[olev:] + dot(vhi, lo)

    @pl.loop(0, cells // LANES)
    def _(b):
        first = pl.multiple_of(b * LANES, LANES)
        here = pl.ds(first, LANES)
        begin = base[0] + first - HALO_O
        place = lax.broadcasted_iota(jnp.int32, (3 * LANES, LANES), 0)
        table = jnp.zeros((3 * LANES, LANES), F32)
        held = jnp.zeros((1, LANES), F32)
        for k in range(sides):
            d = diff[k, :, here]
            held = held + d
            table = table + jnp.where(place == nbr[k, :, here] - begin, d, 0.0)
        hi, lo = split(table)
        window = pl.ds(first, 3 * LANES)
        heads = dot(ext[0, :, window], jnp.concatenate([hi, lo], axis=1))
        lap = heads[:, :LANES] + heads[:, LANES:] + dot(ext[1, :, window], hi)
        wet = sea[:, here] == 1
        for f in range(fields):
            own = ov[f, :, here]
            new = own + (lap[f * olev : (f + 1) * olev] - held * own) + vert[f, :, here]
            res[f, :, here] = jnp.where(wet, new, own)

    out = pltpu.make_async_copy(res, fresh, r_sem.at[0])
    out.start()
    out.wait()


def inner_step(ocean_flag, elem, xt, ue, enbr, coupling, stiffness, metric, vertical, flux):
    rows, width = xt.shape
    fields, points = flux.shape[0], flux.shape[1]
    sides = enbr.shape[0]
    blocks = rows // (2 * LANES)
    return pl.pallas_call(
        inner_kernel,
        out_shape=(
            jax.ShapeDtypeStruct((rows, width), BF16),
            jax.ShapeDtypeStruct((blocks, 4 * LANES, 4 * LANES), BF16),
        ),
        in_specs=[SMEM, SMEM] + [VMEM] * 8,
        out_specs=(VMEM, VMEM),
        scratch_shapes=[
            pltpu.VMEM(((sides + 1) * points, LANES), F32),
            pltpu.VMEM((LANES, LANES), F32),
            pltpu.VMEM((2 * LANES, 2 * LANES), BF16),
            pltpu.VMEM((LANES, LANES), F32),
            pltpu.VMEM((fields, LANES, LANES), F32),
        ],
        compiler_params=params(12),
        cost_estimate=cost(10_000_000_000, 10 << 20),
        name="inner_step",
    )(ocean_flag, elem, xt, ue, enbr, coupling, stiffness, metric, vertical, flux)


def flux_kernel(ocean, dom, owner, block, source, *refs):
    n_tops = len(refs) - 12
    tops = refs[:n_tops]
    weights, coef, sv, flux, sent, fresh, tv, wcat, surf, fl, zv, z_sem = refs[n_tops:]
    pairs = weights.shape[0]
    points, fields = coef.shape[0], flux.shape[0]
    ocean_blocks = sent.shape[0] // n_tops
    chips = n_tops // 2

    @pl.when(ocean[0] == 0)
    def _():
        zv[...] = jnp.zeros_like(zv)
        zeros = copies([(zv, fresh.at[f]) for f in range(fields)], z_sem)
        start(zeros)
        surf[...] = jnp.zeros_like(surf)
        sent[...] = jnp.zeros_like(sent)
        chip, core = dom[0] // 2, dom[0] % 2

        def doubled(rows):
            hi, lo = split(rows)
            eight = jnp.concatenate([hi.astype(F32), lo.astype(F32)], axis=0).astype(BF16)
            return jnp.concatenate([eight, eight], axis=1)

        @pl.loop(0, pairs, unroll=4)
        def _(r):
            hi, lo = split(weights[r])
            wcat[r, :, pl.ds(0, BLK)] = hi
            wcat[r, :, pl.ds(BLK, BLK)] = lo

        for i in range(n_tops):
            tv[i] = tops[i][...]
        for r in range(pairs):
            at = pl.multiple_of(block[r] * BLK, BLK)
            which = owner[r]
            slot = ((which // 2) ^ chip) + jnp.where(which % 2 == core, 0, chips)
            rows = doubled(tv[slot, :, pl.ds(at, BLK)])
            out = dot_t(rows, wcat[r])
            surf[source[r]] += out[:fields] + out[fields:]

        for p in range(points):
            value = coef[pl.ds(p, 1), :] * (sv[:, p, :] - surf[p])
            fl[p] = value
            flux[:, p, :] = value

        for r in range(pairs):
            rows = doubled(fl[source[r]])
            both = jnp.concatenate([wcat[r, :, pl.ds(0, BLK)], wcat[r, :, pl.ds(BLK, BLK)]], axis=0)
            out = dot(rows, both)
            sent[owner[r] * ocean_blocks + block[r]] += out[:fields] + out[fields:]
        wait(zeros)


def fluxes(ocean_flag, dom, owner, block, source, tops, weights, coef, surface, ocean_shape, ocean_blocks):
    fields, points, elems = surface.shape
    pairs = weights.shape[0]
    n = len(tops)
    return pl.pallas_call(
        flux_kernel,
        out_shape=(
            jax.ShapeDtypeStruct((fields, points, elems), F32),
            jax.ShapeDtypeStruct((n * ocean_blocks, fields, BLK), F32),
            jax.ShapeDtypeStruct(ocean_shape, F32),
        ),
        in_specs=[SMEM] * 5 + [VMEM] * (n + 3),
        out_specs=(VMEM, VMEM, HBM),
        scratch_shapes=[
            pltpu.VMEM((n,) + tops[0].shape, F32),
            pltpu.VMEM((pairs, BLK, 2 * BLK), BF16),
            pltpu.VMEM((points, fields, BLK), F32),
            pltpu.VMEM((points, fields, BLK), F32),
            pltpu.VMEM(ocean_shape[1:], F32),
            pltpu.SemaphoreType.DMA((fields,)),
        ],
        compiler_params=params(8),
        cost_estimate=cost(2_500_000_000, 2 << 20),
        name="fluxes",
    )(ocean_flag, dom, owner, block, source, *tops, weights, coef, surface)


def second_kernel(ocean, dom, u, from_core, from_chip, table, metric, vertical, flux, held, out, xhl, wa, mt, xv, ov, o_sem):
    del held
    fields, points = flux.shape[0], flux.shape[1]
    rows, levels = xv.shape[1], xv.shape[2]
    blocks = table.shape[0]
    edge = 2 * LANES

    @pl.when(ocean[0] == 0)
    def _():
        prepare(metric, vertical, wa, mt)
        edge_windows(dom, xhl, u, from_core, from_chip)

        def step(b, window):
            first = b * edge if isinstance(b, int) else pl.multiple_of(b * edge, edge)

            def store(f, value):
                xv[f, pl.ds(first, edge), :] = value

            advance(window, table.at[b], wa, mt, b * 2 * GROUP, points, store, range(fields))

        @pl.loop(1, blocks - 1, step=3)
        def _(start_of):
            for i in range(3):
                b = start_of + i
                step(b, u.at[pl.ds(pl.multiple_of(b * edge - LANES, LANES), 4 * LANES)])

        step(0, xhl.at[pl.ds(0, 4 * LANES)])
        step(blocks - 1, xhl.at[pl.ds(4 * LANES, 4 * LANES)])
        outs = copies([(ov.at[f], out.at[f]) for f in range(fields)], o_sem)
        for f in range(fields):
            for p in range(points):
                cols = [xv[f, pl.ds(g * LANES + p * GROUP, GROUP), :] for g in range(LANES // GROUP)]
                ov[f, pl.ds(p, LANES, stride=points), :] = jnp.concatenate(cols, axis=0).T
            last = pl.ds((levels - 1) * points, points)
            ov[f, last, :] = ov[f, last, :] - 0.5 * flux[f]
            outs[f].start()
        wait(outs)


def second_step(ocean_flag, dom, u, from_core, from_chip, table, metric, vertical, flux, zeroed, levels):
    fields, points = flux.shape[0], flux.shape[1]
    rows, width = u.shape
    return pl.pallas_call(
        second_kernel,
        out_shape=jax.ShapeDtypeStruct((fields, levels * points, LANES), F32),
        in_specs=[SMEM, SMEM] + [VMEM] * 7 + [HBM],
        out_specs=HBM,
        input_output_aliases={9: 0},
        scratch_shapes=[
            pltpu.VMEM((8 * LANES, width), BF16),
            pltpu.VMEM((2 * LANES, 2 * LANES), BF16),
            pltpu.VMEM((LANES, LANES), F32),
            pltpu.VMEM((fields, rows, levels), F32),
            pltpu.VMEM((fields, levels * points, LANES), F32),
            pltpu.SemaphoreType.DMA((fields,)),
        ],
        compiler_params=params(20),
        cost_estimate=cost(10000000000, 12 << 20),
        name="second_step",
    )(ocean_flag, dom, u, from_core, from_chip, table, metric, vertical, flux, zeroed)


def blank_kernel(out):
    del out


def blank(shape):
    return pl.pallas_call(
        blank_kernel, out_shape=jax.ShapeDtypeStruct(shape, F32), out_specs=HBM, compiler_params=params(4), cost_estimate=cost(0, 1024), name="blank"
    )()


def top_kernel(ocean, o, top, tv, sem):
    fields = top.shape[0]

    @pl.when(ocean[0] != 0)
    def _():
        loads = copies([(o.at[f, pl.ds(0, 8)], tv.at[f]) for f in range(fields)], sem)
        start(loads)
        wait(loads)
        for f in range(fields):
            top[pl.ds(f, 1), :] = tv[f, pl.ds(0, 1), :]


def top_rows(ocean_flag, ocean):
    fields, olev, cells = ocean.shape
    return pl.pallas_call(
        top_kernel,
        out_shape=jax.ShapeDtypeStruct((fields, cells), F32),
        in_specs=[SMEM, ANY],
        out_specs=VMEM,
        scratch_shapes=[pltpu.VMEM((fields, 8, cells), F32), pltpu.SemaphoreType.DMA((fields,))],
        compiler_params=params(TURN),
        cost_estimate=cost(0, 1 << 16),
        name="top_rows",
    )(ocean_flag, ocean)


def gather_kernel(dom, *refs):
    parts, (keep, give) = refs[:-2], refs[-2:]
    half, per = keep.shape[0], keep.shape[1]
    for core, out in ((0, keep), (1, give)):
        for s in range(half):
            at = pl.ds((dom[0] ^ (2 * s + core)) * per, per)
            total = parts[0][at]
            for part in parts[1:]:
                total = total + part[at]
            out[s] = total


def gather_sent(dom, parts, n_dom):
    total, fields, blk = parts[0].shape
    shape = jax.ShapeDtypeStruct((n_dom // 2, total // n_dom, fields, blk), F32)
    return pl.pallas_call(
        gather_kernel,
        out_shape=(shape, shape),
        in_specs=[SMEM] + [VMEM] * len(parts),
        out_specs=(VMEM, VMEM),
        compiler_params=params(6),
        name="gather_sent",
    )(dom, *parts)


def pair_kernel(same, other, *outs):
    for s, out in enumerate(outs):
        out[...] = same[s] + other[s]


def pair_sums(same, other):
    chips = same.shape[0]
    return pl.pallas_call(
        pair_kernel,
        out_shape=(jax.ShapeDtypeStruct(same.shape[1:], F32),) * chips,
        in_specs=[VMEM, VMEM],
        out_specs=(VMEM,) * chips,
        compiler_params=params(4),
        cost_estimate=cost(0, 1 << 16),
        name="pair_sums",
    )(same, other)


def add_kernel(*refs):
    parts, out = refs[:-1], refs[-1]
    total = parts[0][...]
    for part in parts[1:]:
        total = total + part[...]
    out[...] = total


def add_up(parts):
    return pl.pallas_call(
        add_kernel,
        out_shape=jax.ShapeDtypeStruct(parts[0].shape, F32),
        in_specs=[VMEM] * len(parts),
        out_specs=VMEM,
        compiler_params=params(4),
        cost_estimate=cost(0, 1 << 16),
        name="add_up",
    )(*parts)


def finish_kernel(ocean, fresh, sea, total, out, sv, pv, rows_v, in_sem, out_sem):
    del fresh
    fields, cells = rows_v.shape[0], rows_v.shape[2]

    @pl.when(ocean[0] != 0)
    def _():
        loads = copies([(out.at[f, pl.ds(0, 8)], rows_v.at[f]) for f in range(fields)] + [(total, pv), (sea, sv)], in_sem)
        start(loads)
        wait(loads)
        for b in range(cells // BLK):
            here = pl.ds(b * BLK, BLK)
            part = jnp.where(sv[:, here] == 1, 0.5 * pv[b], 0.0)
            for f in range(fields):
                rows_v[f, pl.ds(0, 1), here] = rows_v[f, pl.ds(0, 1), here] + part[f : f + 1]
        stores = copies([(rows_v.at[f], out.at[f, pl.ds(0, 8)]) for f in range(fields)], out_sem)
        start(stores)
        wait(stores)


def finish(ocean_flag, fresh, total, sea):
    fields, olev, cells = fresh.shape
    return pl.pallas_call(
        finish_kernel,
        out_shape=jax.ShapeDtypeStruct(fresh.shape, F32),
        in_specs=[SMEM, HBM, ANY, ANY],
        out_specs=HBM,
        input_output_aliases={1: 0},
        scratch_shapes=[
            pltpu.VMEM(sea.shape, jnp.int32),
            pltpu.VMEM(total.shape, F32),
            pltpu.VMEM((fields, 8, cells), F32),
            pltpu.SemaphoreType.DMA((fields + 2,)),
            pltpu.SemaphoreType.DMA((fields,)),
        ],
        compiler_params=params(8),
        cost_estimate=cost(0, 1 << 16),
        name="finish_ocean",
    )(ocean_flag, fresh, sea, total)


def local(
    atm_state,
    elem_nbr,
    elem_metric,
    bulk_coef,
    stiffness,
    coupling,
    atm_vertical,
    ocean_state,
    cell_nbr,
    cell_diff,
    ocean_vertical,
    sea_mask,
    pair_owner,
    pair_block,
    pair_src,
    remap_weight,
):
    n_comp = lax.axis_size("comp")
    n_dom = lax.axis_size("dom")
    comp_index = lax.axis_index("comp")
    dom_index = lax.axis_index("dom")
    live = n_comp - 1
    chips = n_dom // 2
    state = atm_state[0]
    ocean = ocean_state[0]
    fields, levels, points, elems = state.shape
    cells = ocean.shape[2]
    ocean_blocks = cells // BLK
    one = lambda value: value.astype(jnp.int32).reshape(1)
    flag = one(comp_index == live)
    comp = one(comp_index)
    dom = one(dom_index)
    elem_base = one((comp_index * n_dom + dom_index) * elems)
    cell_base = one(dom_index * cells)

    both = ("comp", "dom")
    swapped = [(d, d ^ 1) for d in range(n_dom)]
    between = [(i, i + 1) for i in range(1, live * n_dom - 1, 2)]
    atm_chips = between + [(j, i) for i, j in between]
    between = [(live * n_dom + i, live * n_dom + i + 1) for i in range(1, n_dom - 1, 2)]
    all_chips = atm_chips + between + [(j, i) for i, j in between]

    def from_ocean(c):
        return [(live * n_dom + d, c * n_dom + d) for d in range(n_dom)]

    def to_ocean(c):
        return [(j, i) for i, j in from_ocean(c)]

    def among_ocean(pairs):
        return [(live * n_dom + a, live * n_dom + b) for a, b in pairs]

    is_ocean = comp_index == live
    chips = n_dom // 2

    def shifted(by):
        return [(d, d ^ (2 * by)) for d in range(n_dom)]

    top = top_rows(flag, ocean)
    brought = [lax.ppermute(top, both, from_ocean(c)) for c in range(live)]
    xt, to_core, to_chip, surface, zeroed = turn(flag, dom, state, ocean)
    brought, to_core, to_chip = lax.optimization_barrier((brought, to_core, to_chip))
    got = sum(brought)
    got, to_core, to_chip = lax.optimization_barrier((got, to_core, to_chip))
    near = [got] + [lax.ppermute(got, "dom", shifted(s)) for s in range(1, chips)]
    tops = near + [lax.ppermute(part, "dom", swapped) for part in near]
    from_core = lax.ppermute(to_core, "dom", swapped)
    from_chip = lax.ppermute(to_chip, both, all_chips)
    metric = elem_metric[0]

    operators = (elem_nbr[0], coupling.reshape(-1, points), stiffness, metric, atm_vertical)
    flux, sent, fresh = fluxes(
        flag,
        dom,
        pair_owner[0, :, 0],
        pair_block[0],
        pair_src[0],
        tops,
        remap_weight[0],
        bulk_coef[0],
        surface,
        ocean.shape,
        ocean_blocks,
    )
    parts = [lax.ppermute(sent, both, to_ocean(c)) for c in range(live)]
    ue, to_core, to_chip, fresh = edge_step(
        flag,
        dom,
        elem_base,
        cell_base,
        xt,
        from_core,
        from_chip,
        *operators,
        flux,
        ocean,
        cell_nbr[0][:, None],
        cell_diff[0][:, None],
        sea_mask,
        ocean_vertical,
        fresh,
    )
    from_chip2 = lax.ppermute(to_chip, both, atm_chips)
    from_core2 = lax.ppermute(to_core, "dom", swapped)
    u, table = inner_step(flag, elem_base, xt, ue, *operators, flux)
    atm_next = second_step(flag, dom, u, from_core2, from_chip2, table, metric, atm_vertical, flux, zeroed, levels)

    parts, atm_next = lax.optimization_barrier((parts, atm_next))

    def reduce_parts():
        same, other = gather_sent(dom, parts, n_dom)
        pieces = pair_sums(same, lax.ppermute(other, both, among_ocean(swapped)))
        mine = [pieces[0]]
        for s in range(1, chips):
            mine.append(lax.ppermute(pieces[s], both, among_ocean(shifted(s))))
        return add_up(mine)

    total = lax.cond(is_ocean, reduce_parts, lambda: blank((ocean_blocks, fields, BLK)))
    ocean_next = finish(flag, fresh, total, sea_mask)
    return (atm_next.reshape(state.shape)[None], ocean_next[None])


def solution(mesh):
    in_specs = (
        P("comp", None, None, None, "dom"),
        P("comp", None, "dom"),
        P("comp", None, "dom"),
        P("comp", None, "dom"),
        P(),
        P(),
        P(),
        P("comp", None, None, "dom"),
        P("comp", None, "dom"),
        P("comp", None, "dom"),
        P(),
        P("comp", "dom"),
        P("comp", "dom", None),
        P("comp", "dom"),
        P("comp", "dom"),
        P("comp", "dom", None, None),
    )
    out_specs = (P("comp", None, None, None, "dom"), P("comp", None, None, "dom"))
    return jax.shard_map(local, mesh=mesh, in_specs=in_specs, out_specs=out_specs, check_vma=False)
```

```python
import functools

import jax
import jax.numpy as jnp
from jax import lax
from jax.experimental import pallas as pl
from jax.experimental.pallas import tpu as pltpu
from jax.sharding import PartitionSpec as P

RIM = 8
BLK = 128
HALO_O = 128
LANES = 128
GROUP = 8
TURN = 60

F32 = jnp.float32
BF16 = jnp.bfloat16
ANY = pl.BlockSpec(memory_space=pl.ANY)
HBM = pl.BlockSpec(memory_space=pltpu.HBM)
SMEM = pl.BlockSpec(memory_space=pltpu.SMEM)
VMEM = pl.BlockSpec(memory_space=pltpu.VMEM)


def params(mib):
    return pltpu.CompilerParams(vmem_limit_bytes=mib << 20)


def cost(flops, moved):
    return pl.CostEstimate(flops=flops, bytes_accessed=moved, transcendentals=0)


def split(x):
    hi = x.astype(BF16)
    return hi, (x - hi.astype(F32)).astype(BF16)


def dot(a, b):
    return jnp.dot(a, b, preferred_element_type=F32)


def dot_t(a, b):
    return lax.dot_general(a, b, (((1,), (1,)), ((), ())), preferred_element_type=F32)


def turned(rows):
    n = rows.shape[0]
    if n < LANES:
        rows = jnp.concatenate([rows, jnp.zeros((LANES - n, LANES), rows.dtype)], axis=0)
    return rows.T


OCEAN, DOM, ELEM, CELL = range(4)


def copies(pairs, sem):
    return [pltpu.make_async_copy(a, b, sem.at[i]) for i, (a, b) in enumerate(pairs)]


def start(many):
    for one in many:
        one.start()


def wait(many):
    for one in many:
        one.wait()


def hand_out(dom, low_high, to_core, to_chip):
    core = dom[0] % 2
    to_core[...] = low_high[1 - core]
    to_chip[...] = low_high[core]


def take_in(dom, from_core, from_chip, f):
    first = dom[0] % 2 == 0
    a, b = from_core[f], from_chip[f]
    return jnp.where(first, b, a), jnp.where(first, a, b)


def turn_kernel(ocean, dom, x, o, xt, to_core, to_chip, surface, xv, tv, hv, in_sem, out_sem, o_sem):
    fields, points = xv.shape[0], 16
    olev, cells = o.shape[1], o.shape[2]
    groups = LANES // GROUP

    @pl.when(ocean[0] == 0)
    def _():
        loads = copies([(x.at[f], xv.at[f]) for f in range(fields)], in_sem)
        start(loads)
        outs = []
        levels = xv.shape[1] // points
        for f in range(fields):
            loads[f].wait()
            surface[f] = xv[f, pl.ds((levels - 1) * points, points), :]
            hi_at, lo_at = pl.ds(f * LANES, LANES), pl.ds((fields + f) * LANES, LANES)
            for q in range(0, points, 2):
                one = xv[f, pl.ds(q, LANES, stride=points), :].T
                two = xv[f, pl.ds(q + 1, LANES, stride=points), :].T
                for g in range(groups):
                    part = slice(g * GROUP, (g + 1) * GROUP)
                    rows = jnp.concatenate([one[part], two[part]], axis=0)
                    if g == 0:
                        hv[0, f, pl.ds(q * GROUP, 2 * GROUP), :] = rows
                    if g == groups - 1:
                        hv[1, f, pl.ds(q * GROUP, 2 * GROUP), :] = rows
                    hi, lo = split(rows)
                    at = pl.ds((g * points + q) * GROUP, 2 * GROUP)
                    tv[at, hi_at] = hi
                    tv[at, lo_at] = lo
            outs += copies([(tv.at[:, at], xt.at[:, at]) for at in (hi_at, lo_at)], out_sem.at[f])
            start(outs[-2:])
        hand_out(dom, hv, to_core, to_chip)
        wait(outs)

    @pl.when(ocean[0] != 0)
    def _():
        pairs = []
        for f in range(fields):
            pairs.append((o.at[f, :, pl.ds(0, HALO_O)], hv.at[0, f, pl.ds(0, olev)]))
            pairs.append((o.at[f, :, pl.ds(cells - HALO_O, HALO_O)], hv.at[1, f, pl.ds(0, olev)]))
        loads = copies(pairs, o_sem)
        start(loads)
        wait(loads)
        hand_out(dom, hv, to_core, to_chip)


def turn(ocean_flag, dom, state, ocean):
    fields, levels, points, elems = state.shape
    rows = points * elems
    halo = jax.ShapeDtypeStruct((fields, LANES, LANES), F32)
    return pl.pallas_call(
        turn_kernel,
        out_shape=(
            jax.ShapeDtypeStruct((rows, 2 * fields * LANES), BF16),
            halo,
            halo,
            jax.ShapeDtypeStruct((fields, points, elems), F32),
        ),
        in_specs=[SMEM, SMEM, ANY, ANY],
        out_specs=(ANY, VMEM, VMEM, VMEM),
        scratch_shapes=[
            pltpu.VMEM((fields, levels * points, elems), F32),
            pltpu.VMEM((rows, 2 * fields * LANES), BF16),
            pltpu.VMEM((2, fields, LANES, LANES), F32),
            pltpu.SemaphoreType.DMA((fields,)),
            pltpu.SemaphoreType.DMA((fields, 2)),
            pltpu.SemaphoreType.DMA((2 * fields,)),
        ],
        compiler_params=params(TURN),
        cost_estimate=cost(2000000000, 9 << 20),
        name="turn_state",
    )(ocean_flag, dom, state.reshape(fields, levels * points, elems), ocean)


def prepare_table(base, nbr, coupling, stiffness, cx, nt):
    points = stiffness.shape[0]
    nt[...] = turned((nbr[...] - base[0]).astype(F32))
    spread = lax.broadcasted_iota(jnp.int32, (points, LANES), 1) // GROUP
    spread = (spread == lax.broadcasted_iota(jnp.int32, (points, LANES), 0)).astype(F32)
    for ops, first in ((coupling, 0), (stiffness, coupling.shape[0])):
        cx[pl.ds(first, ops.shape[0]), :] = jnp.dot(
            ops[...], spread, precision=lax.Precision.HIGHEST, preferred_element_type=F32
        )


def build_table(block, table, slot, cx, nt, sides, points):
    lane = lax.broadcasted_iota(jnp.int32, (GROUP, LANES), 1) % GROUP
    lane_f = lane.astype(F32)
    same = lane == lax.broadcasted_iota(jnp.int32, (GROUP, LANES), 0)
    zero = jnp.zeros((LANES, LANES), BF16)
    for g in range(2):
        first = pl.multiple_of(block * 2 * GROUP + g * GROUP, GROUP)
        own = nt[pl.ds(first, GROUP), :]
        cols = [jnp.broadcast_to(own[:, s : s + 1], (GROUP, LANES)) for s in range(sides)]
        masks = {}
        for h in range(4):
            if h - g not in (0, 1, 2):
                at = pl.ds(h * LANES, LANES)
                table[slot, pl.ds(g * LANES, LANES), at] = zero
                table[slot, pl.ds((2 + g) * LANES, LANES), at] = zero
                continue
            begin = jnp.asarray(block * 2 * GROUP + (h - 1) * GROUP, jnp.int32).astype(F32)
            masks[h] = [col - begin == lane_f for col in cols]
        for p in range(0, points, 2):
            rows = [
                [jnp.broadcast_to(cx[pl.ds(s * points + pp, 1), :], (GROUP, LANES)) for s in range(sides + 1)]
                for pp in (p, p + 1)
            ]
            for h in masks:
                pair = []
                for row in rows:
                    total = jnp.where(masks[h][0], row[0], 0.0)
                    for s in range(1, sides):
                        total = total + jnp.where(masks[h][s], row[s], 0.0)
                    if h == g + 1:
                        total = total + jnp.where(same, row[sides], 0.0)
                    pair.append(total)
                top, rest = split(jnp.concatenate(pair, axis=0))
                at = pl.ds(h * LANES, LANES)
                table[slot, pl.ds(g * LANES + p * GROUP, 2 * GROUP), at] = top
                table[slot, pl.ds((2 + g) * LANES + p * GROUP, 2 * GROUP), at] = rest


def put_split(xhl, at, f, fields, x):
    hi, lo = split(x)
    xhl[at, pl.ds(f * LANES, LANES)] = hi
    xhl[at, pl.ds((fields + f) * LANES, LANES)] = lo


def columns(turned_rows, first, points):
    pieces = []
    for g in range(2):
        own = turned_rows[pl.ds(pl.multiple_of(first + g * GROUP, GROUP), GROUP), :]
        pieces += [jnp.broadcast_to(own[:, q : q + 1], (GROUP, LANES)) for q in range(points)]
    return jnp.concatenate(pieces, axis=0)


def advance(window, table, wa, mt, element, points, store, chosen):
    fields = window.shape[1] // (2 * LANES)
    rows = 2 * LANES
    n = len(chosen)
    heads = dot(table[...], window[:, pl.ds(chosen[0] * LANES, n * LANES)])
    rest = dot(table[pl.ds(0, rows), :], window[:, pl.ds((fields + chosen[0]) * LANES, n * LANES)])
    inner = pl.ds(LANES, rows)
    hi = [window[inner, f * LANES : (f + 1) * LANES] for f in chosen]
    lo = [window[inner, (fields + f) * LANES : (fields + f + 1) * LANES] for f in chosen]
    v = dot(jnp.concatenate([jnp.concatenate([a, b], axis=1) for a, b in zip(hi, lo)], axis=0), wa[...])
    m = columns(mt, element, points)
    for i, f in enumerate(chosen):
        at = slice(i * LANES, (i + 1) * LANES)
        own = slice(i * rows, (i + 1) * rows)
        tend = heads[:rows, at] + heads[rows:, at] + rest[:, at] + v[own, :LANES] + v[own, LANES:]
        store(f, hi[i].astype(F32) + lo[i].astype(F32) + m * tend)


def prepare(metric, vertical, wa, mt):
    mt[...] = turned(metric[...])
    hi, lo = split(vertical[...].T)
    wa[pl.ds(0, LANES), pl.ds(0, LANES)] = hi
    wa[pl.ds(LANES, LANES), pl.ds(0, LANES)] = hi
    wa[pl.ds(0, LANES), pl.ds(LANES, LANES)] = lo
    wa[pl.ds(LANES, LANES), pl.ds(LANES, LANES)] = jnp.zeros((LANES, LANES), BF16)


def put_flux(ft, flux):
    for f in range(flux.shape[0]):
        ft[f] = turned(-0.5 * flux[f])


def edge_windows(dom, xhl, x, from_core, from_chip):
    fields = from_core.shape[0]
    rows = x.shape[0]
    side = 3 * LANES
    xhl[pl.ds(LANES, side), :] = x[pl.ds(0, side), :]
    xhl[pl.ds(4 * LANES, side), :] = x[pl.ds(rows - side, side), :]
    for f in range(fields):
        left, right = take_in(dom, from_core, from_chip, f)
        put_split(xhl, pl.ds(0, LANES), f, fields, left)
        put_split(xhl, pl.ds(7 * LANES, LANES), f, fields, right)


def edge_kernel(
    ocean, dom, elem, base, xt, from_core, from_chip, enbr, coupling, stiffness, metric, vertical, flux,
    o, nbr, diff, sea, overt, held,
    u, to_core, to_chip, fresh, zeroed,
    table, cx, nt, xhl, hv, wa, mt, ft, ov, ext, res, vert, zv, o_sem, r_sem, z_sem,
):
    del held
    fields, points = flux.shape[0], flux.shape[1]
    blocks = xt.shape[0] // (2 * LANES)
    sides = enbr.shape[0]

    @pl.when(ocean[0] == 0)
    def _():
        prepare_table(elem, enbr, coupling, stiffness, cx, nt)
        for i in range(2):
            build_table(i * (blocks - 1), table, i, cx, nt, sides, points)
        prepare(metric, vertical, wa, mt)
        put_flux(ft, flux)
        edge_windows(dom, xhl, xt, from_core, from_chip)
        last_lane = lax.broadcasted_iota(jnp.int32, (2 * LANES, LANES), 1) == LANES - 1
        for i in range(2):
            b = i * (blocks - 1)
            element = b * 2 * GROUP

            def store(f, value):
                value = value + jnp.where(last_lane, columns(ft.at[f], element, points), 0.0)
                put_split(u, pl.ds(i * 2 * LANES, 2 * LANES), f, fields, value)
                hv[i, f] = value[:LANES] if i == 0 else value[LANES:]

            advance(
                xhl.at[pl.ds(i * 4 * LANES, 4 * LANES)], table.at[i], wa, mt, element, points, store, range(fields)
            )
        hand_out(dom, hv, to_core, to_chip)

    @pl.when(ocean[0] != 0)
    def _():
        load = pltpu.make_async_copy(o, ov, o_sem.at[0])
        load.start()
        zv[...] = jnp.zeros_like(zv)
        zeros = copies([(zv, zeroed.at[f]) for f in range(fields)], z_sem)
        start(zeros)
        ocean_part(dom, base, load, from_core, from_chip, nbr, diff, sea, overt, fresh, ov, ext, res, vert, r_sem)
        wait(zeros)


def edge_step(
    ocean_flag, dom, elem, base, xt, from_core, from_chip, enbr, coupling, stiffness, metric, vertical, flux,
    ocean, nbr, diff, sea, overt, fresh,
):
    width = xt.shape[1]
    points = stiffness.shape[0]
    sides = enbr.shape[0]
    fields = flux.shape[0]
    olev, cells = ocean.shape[1], ocean.shape[2]
    halo = jax.ShapeDtypeStruct((fields, LANES, LANES), F32)
    return pl.pallas_call(
        edge_kernel,
        out_shape=(
            jax.ShapeDtypeStruct((4 * LANES, width), BF16),
            halo,
            halo,
            jax.ShapeDtypeStruct(ocean.shape, F32),
            jax.ShapeDtypeStruct((fields,) + xt.shape[:1] + (LANES,), F32),
        ),
        in_specs=[SMEM] * 4 + [VMEM] * 9 + [HBM] + [VMEM] * 4 + [HBM],
        out_specs=(VMEM, VMEM, VMEM, HBM, HBM),
        input_output_aliases={18: 3},
        scratch_shapes=[
            pltpu.VMEM((2, 4 * LANES, 4 * LANES), BF16),
            pltpu.VMEM(((sides + 1) * points, LANES), F32),
            pltpu.VMEM((LANES, LANES), F32),
            pltpu.VMEM((8 * LANES, width), BF16),
            pltpu.VMEM((2, fields, LANES, LANES), F32),
            pltpu.VMEM((2 * LANES, 2 * LANES), BF16),
            pltpu.VMEM((LANES, LANES), F32),
            pltpu.VMEM((fields, LANES, LANES), F32),
            pltpu.VMEM(ocean.shape, F32),
            pltpu.VMEM((2, fields * olev, cells + 2 * HALO_O), BF16),
            pltpu.VMEM(ocean.shape, F32),
            pltpu.VMEM(ocean.shape, F32),
            pltpu.VMEM(xt.shape[:1] + (LANES,), F32),
            pltpu.SemaphoreType.DMA((1,)),
            pltpu.SemaphoreType.DMA((1,)),
            pltpu.SemaphoreType.DMA((fields,)),
        ],
        compiler_params=params(20),
        cost_estimate=cost(4000000000, 3 << 20),
        name="edge_step",
    )(
        ocean_flag, dom, elem, base, xt, from_core, from_chip, enbr, coupling, stiffness, metric, vertical, flux,
        ocean, nbr, diff, sea, overt, fresh,
    )


def inner_kernel(ocean, elem, xt, ue, enbr, coupling, stiffness, metric, vertical, flux, u, table, xv, cx, nt, wa, mt, ft):
    fields, points = flux.shape[0], flux.shape[1]
    sides = enbr.shape[0]
    rows = xt.shape[0]
    blocks = table.shape[0]
    edge = 2 * LANES

    @pl.when(ocean[0] == 0)
    def _():
        prepare_table(elem, enbr, coupling, stiffness, cx, nt)
        for b in range(2):
            build_table(b, table, b, cx, nt, sides, points)
        prepare(metric, vertical, wa, mt)
        put_flux(ft, flux)
        u[pl.ds(0, edge), :] = ue[pl.ds(0, edge), :]
        u[pl.ds(rows - edge, edge), :] = ue[pl.ds(edge, edge), :]
        last_lane = lax.broadcasted_iota(jnp.int32, (edge, LANES), 1) == LANES - 1

        @pl.loop(1, blocks - 1, step=3)
        def _(start_of):
            for i in range(3):
                b = start_of + i
                first = pl.multiple_of(b * edge, edge)
                element = b * 2 * GROUP

                def store(f, value):
                    value = value + jnp.where(last_lane, columns(ft.at[f], element, points), 0.0)
                    put_split(u, pl.ds(first, edge), f, fields, value)

                window = xt.at[pl.ds(pl.multiple_of(first - LANES, LANES), 4 * LANES)]
                advance(window, table.at[b], wa, mt, element, points, store, range(fields))
                build_table(b + 1, table, b + 1, cx, nt, sides, points)

        @pl.loop(1, blocks - 1, step=3)
        def _(start_of):
            for i in range(3):
                b = start_of + i
                first = pl.multiple_of(b * edge, edge)

                def store(f, value):
                    xv[f, pl.ds(first, edge), :] = value

                window = u.at[pl.ds(pl.multiple_of(first - LANES, LANES), 4 * LANES)]
                advance(window, table.at[b], wa, mt, b * 2 * GROUP, points, store, range(fields))


def ocean_part(dom, base, load, from_core, from_chip, nbr, diff, sea, overt, fresh, ov, ext, res, vert, r_sem):
    fields, olev, cells = ov.shape
    sides = nbr.shape[0]
    for f in range(fields):
        rows = pl.ds(f * olev, olev)
        left, right = take_in(dom, from_core, from_chip, f)
        for at, value in ((0, left[:olev]), (HALO_O + cells, right[:olev])):
            hi, lo = split(value)
            ext[0, rows, pl.ds(at, HALO_O)] = hi
            ext[1, rows, pl.ds(at, HALO_O)] = lo
    vhi, vlo = split(overt[...])
    both = jnp.concatenate([vhi, vlo], axis=0)
    load.wait()
    for f in range(fields):
        rows = pl.ds(f * olev, olev)
        hi, lo = split(ov[f])
        ext[0, rows, pl.ds(HALO_O, cells)] = hi
        ext[1, rows, pl.ds(HALO_O, cells)] = lo
        v = dot(both, hi)
        vert[f] = v[:olev] + v[olev:] + dot(vhi, lo)

    @pl.loop(0, cells // LANES)
    def _(b):
        first = pl.multiple_of(b * LANES, LANES)
        here = pl.ds(first, LANES)
        begin = base[0] + first - HALO_O
        place = lax.broadcasted_iota(jnp.int32, (3 * LANES, LANES), 0)
        table = jnp.zeros((3 * LANES, LANES), F32)
        held = jnp.zeros((1, LANES), F32)
        for k in range(sides):
            d = diff[k, :, here]
            held = held + d
            table = table + jnp.where(place == nbr[k, :, here] - begin, d, 0.0)
        hi, lo = split(table)
        window = pl.ds(first, 3 * LANES)
        heads = dot(ext[0, :, window], jnp.concatenate([hi, lo], axis=1))
        lap = heads[:, :LANES] + heads[:, LANES:] + dot(ext[1, :, window], hi)
        wet = sea[:, here] == 1
        for f in range(fields):
            own = ov[f, :, here]
            new = own + (lap[f * olev : (f + 1) * olev] - held * own) + vert[f, :, here]
            res[f, :, here] = jnp.where(wet, new, own)

    out = pltpu.make_async_copy(res, fresh, r_sem.at[0])
    out.start()
    out.wait()


def inner_step(ocean_flag, elem, xt, ue, enbr, coupling, stiffness, metric, vertical, flux):
    rows, width = xt.shape
    fields, points = flux.shape[0], flux.shape[1]
    sides = enbr.shape[0]
    blocks = rows // (2 * LANES)
    return pl.pallas_call(
        inner_kernel,
        out_shape=(
            jax.ShapeDtypeStruct((rows, width), BF16),
            jax.ShapeDtypeStruct((blocks, 4 * LANES, 4 * LANES), BF16),
            jax.ShapeDtypeStruct((fields, rows, LANES), F32),
        ),
        in_specs=[SMEM, SMEM] + [VMEM] * 8,
        out_specs=(VMEM, VMEM, VMEM),
        scratch_shapes=[
            pltpu.VMEM(((sides + 1) * points, LANES), F32),
            pltpu.VMEM((LANES, LANES), F32),
            pltpu.VMEM((2 * LANES, 2 * LANES), BF16),
            pltpu.VMEM((LANES, LANES), F32),
            pltpu.VMEM((fields, LANES, LANES), F32),
        ],
        compiler_params=params(12),
        cost_estimate=cost(10_000_000_000, 10 << 20),
        name="inner_step",
    )(ocean_flag, elem, xt, ue, enbr, coupling, stiffness, metric, vertical, flux)


def flux_kernel(ocean, dom, owner, block, source, *refs):
    n_tops = len(refs) - 14
    tops = refs[:n_tops]
    weights, coef, surface, flux, sent, fresh, sv, tv, wcat, surf, fl, zv, z_sem, s_sem = refs[n_tops:]
    pairs = weights.shape[0]
    points, fields = coef.shape[0], flux.shape[0]
    ocean_blocks = sent.shape[0] // n_tops
    chips = n_tops // 2

    @pl.when(ocean[0] == 0)
    def _():
        load = pltpu.make_async_copy(surface, sv, s_sem)
        load.start()
        zv[...] = jnp.zeros_like(zv)
        zeros = copies([(zv, fresh.at[f]) for f in range(fields)], z_sem)
        start(zeros)
        surf[...] = jnp.zeros_like(surf)
        sent[...] = jnp.zeros_like(sent)
        chip, core = dom[0] // 2, dom[0] % 2

        def doubled(rows):
            hi, lo = split(rows)
            eight = jnp.concatenate([hi.astype(F32), lo.astype(F32)], axis=0).astype(BF16)
            return jnp.concatenate([eight, eight], axis=1)

        @pl.loop(0, pairs, unroll=4)
        def _(r):
            hi, lo = split(weights[r])
            wcat[r, :, pl.ds(0, BLK)] = hi
            wcat[r, :, pl.ds(BLK, BLK)] = lo

        for i in range(n_tops):
            tv[i] = tops[i][...]
        for r in range(pairs):
            at = pl.multiple_of(block[r] * BLK, BLK)
            which = owner[r]
            slot = ((which // 2) ^ chip) + jnp.where(which % 2 == core, 0, chips)
            rows = doubled(tv[slot, :, pl.ds(at, BLK)])
            out = dot_t(rows, wcat[r])
            surf[source[r]] += out[:fields] + out[fields:]

        load.wait()
        for p in range(points):
            value = coef[pl.ds(p, 1), :] * (sv[:, p, :] - surf[p])
            fl[p] = value
            flux[:, p, :] = value

        for r in range(pairs):
            rows = doubled(fl[source[r]])
            both = jnp.concatenate([wcat[r, :, pl.ds(0, BLK)], wcat[r, :, pl.ds(BLK, BLK)]], axis=0)
            out = dot(rows, both)
            sent[owner[r] * ocean_blocks + block[r]] += out[:fields] + out[fields:]
        wait(zeros)


def fluxes(ocean_flag, dom, owner, block, source, tops, weights, coef, surface, ocean_shape, ocean_blocks):
    fields, points, elems = surface.shape
    pairs = weights.shape[0]
    n = len(tops)
    return pl.pallas_call(
        flux_kernel,
        out_shape=(
            jax.ShapeDtypeStruct((fields, points, elems), F32),
            jax.ShapeDtypeStruct((n * ocean_blocks, fields, BLK), F32),
            jax.ShapeDtypeStruct(ocean_shape, F32),
        ),
        in_specs=[SMEM] * 5 + [VMEM] * (n + 2) + [ANY],
        out_specs=(VMEM, VMEM, HBM),
        scratch_shapes=[
            pltpu.VMEM((fields, points, elems), F32),
            pltpu.VMEM((n,) + tops[0].shape, F32),
            pltpu.VMEM((pairs, BLK, 2 * BLK), BF16),
            pltpu.VMEM((points, fields, BLK), F32),
            pltpu.VMEM((points, fields, BLK), F32),
            pltpu.VMEM(ocean_shape[1:], F32),
            pltpu.SemaphoreType.DMA((fields,)),
            pltpu.SemaphoreType.DMA,
        ],
        compiler_params=params(8),
        cost_estimate=cost(2_500_000_000, 2 << 20),
        name="fluxes",
    )(ocean_flag, dom, owner, block, source, *tops, weights, coef, surface)


def second_kernel(
    ocean, dom, xv, u, from_core, from_chip, table, metric, vertical, flux, held, out, xhl, wa, mt, xe, ov, o_sem
):
    del held
    fields, points = flux.shape[0], flux.shape[1]
    blocks = table.shape[0]
    levels = xv.shape[2]
    groups = LANES // GROUP
    edge = 2 * LANES

    @pl.when(ocean[0] == 0)
    def _():
        prepare(metric, vertical, wa, mt)
        edge_windows(dom, xhl, u, from_core, from_chip)
        for i in range(2):
            b = i * (blocks - 1)

            def store(f, value):
                xe[f, pl.ds(i * edge, edge), :] = value

            advance(
                xhl.at[pl.ds(i * 4 * LANES, 4 * LANES)], table.at[b], wa, mt, b * 2 * GROUP, points, store, range(fields)
            )
        outs = copies([(ov.at[f], out.at[f]) for f in range(fields)], o_sem)
        for f in range(fields):
            for p in range(points):
                cols = []
                for g in range(groups):
                    if 2 <= g < groups - 2:
                        cols.append(xv[f, pl.ds(g * LANES + p * GROUP, GROUP), :])
                    else:
                        cols.append(xe[f, pl.ds((g % (groups - 4)) * LANES + p * GROUP, GROUP), :])
                ov[f, pl.ds(p, LANES, stride=points), :] = jnp.concatenate(cols, axis=0).T
            last = pl.ds((levels - 1) * points, points)
            ov[f, last, :] = ov[f, last, :] - 0.5 * flux[f]
            outs[f].start()
        wait(outs)


def second_step(ocean_flag, dom, xv, u, from_core, from_chip, table, metric, vertical, flux, zeroed):
    fields, rows, levels = xv.shape
    points = flux.shape[1]
    width = u.shape[1]
    return pl.pallas_call(
        second_kernel,
        out_shape=jax.ShapeDtypeStruct((fields, levels * points, LANES), F32),
        in_specs=[SMEM, SMEM] + [VMEM] * 8 + [HBM],
        out_specs=HBM,
        input_output_aliases={10: 0},
        scratch_shapes=[
            pltpu.VMEM((8 * LANES, width), BF16),
            pltpu.VMEM((2 * LANES, 2 * LANES), BF16),
            pltpu.VMEM((LANES, LANES), F32),
            pltpu.VMEM((fields, 4 * LANES, levels), F32),
            pltpu.VMEM((fields, levels * points, LANES), F32),
            pltpu.SemaphoreType.DMA((fields,)),
        ],
        compiler_params=params(20),
        cost_estimate=cost(10_000_000_000, 12 << 20),
        name="second_step",
    )(ocean_flag, dom, xv, u, from_core, from_chip, table, metric, vertical, flux, zeroed)


def blank_kernel(out):
    del out


def blank(shape):
    return pl.pallas_call(
        blank_kernel, out_shape=jax.ShapeDtypeStruct(shape, F32), out_specs=HBM, compiler_params=params(4), cost_estimate=cost(0, 1024), name="blank"
    )()


def top_kernel(ocean, o, top, tv, sem):
    fields = top.shape[0]

    @pl.when(ocean[0] != 0)
    def _():
        loads = copies([(o.at[f, pl.ds(0, 8)], tv.at[f]) for f in range(fields)], sem)
        start(loads)
        wait(loads)
        for f in range(fields):
            top[pl.ds(f, 1), :] = tv[f, pl.ds(0, 1), :]


def top_rows(ocean_flag, ocean):
    fields, olev, cells = ocean.shape
    return pl.pallas_call(
        top_kernel,
        out_shape=jax.ShapeDtypeStruct((fields, cells), F32),
        in_specs=[SMEM, ANY],
        out_specs=VMEM,
        scratch_shapes=[pltpu.VMEM((fields, 8, cells), F32), pltpu.SemaphoreType.DMA((fields,))],
        compiler_params=params(TURN),
        cost_estimate=cost(0, 1 << 16),
        name="top_rows",
    )(ocean_flag, ocean)


def gather_kernel(dom, *refs):
    parts, (keep, give) = refs[:-2], refs[-2:]
    half, per = keep.shape[0], keep.shape[1]
    for core, out in ((0, keep), (1, give)):
        for s in range(half):
            at = pl.ds((dom[0] ^ (2 * s + core)) * per, per)
            total = parts[0][at]
            for part in parts[1:]:
                total = total + part[at]
            out[s] = total


def gather_sent(dom, parts, n_dom):
    total, fields, blk = parts[0].shape
    shape = jax.ShapeDtypeStruct((n_dom // 2, total // n_dom, fields, blk), F32)
    return pl.pallas_call(
        gather_kernel,
        out_shape=(shape, shape),
        in_specs=[SMEM] + [VMEM] * len(parts),
        out_specs=(VMEM, VMEM),
        compiler_params=params(6),
        name="gather_sent",
    )(dom, *parts)


def pair_kernel(same, other, *outs):
    for s, out in enumerate(outs):
        out[...] = same[s] + other[s]


def pair_sums(same, other):
    chips = same.shape[0]
    return pl.pallas_call(
        pair_kernel,
        out_shape=(jax.ShapeDtypeStruct(same.shape[1:], F32),) * chips,
        in_specs=[VMEM, VMEM],
        out_specs=(VMEM,) * chips,
        compiler_params=params(4),
        cost_estimate=cost(0, 1 << 16),
        name="pair_sums",
    )(same, other)


def add_kernel(*refs):
    parts, out = refs[:-1], refs[-1]
    total = parts[0][...]
    for part in parts[1:]:
        total = total + part[...]
    out[...] = total


def add_up(parts):
    return pl.pallas_call(
        add_kernel,
        out_shape=jax.ShapeDtypeStruct(parts[0].shape, F32),
        in_specs=[VMEM] * len(parts),
        out_specs=VMEM,
        compiler_params=params(4),
        cost_estimate=cost(0, 1 << 16),
        name="add_up",
    )(*parts)


def finish_kernel(ocean, fresh, sea, total, out, sv, pv, rows_v, in_sem, out_sem):
    del fresh
    fields, cells = rows_v.shape[0], rows_v.shape[2]

    @pl.when(ocean[0] != 0)
    def _():
        loads = copies([(out.at[f, pl.ds(0, 8)], rows_v.at[f]) for f in range(fields)] + [(total, pv), (sea, sv)], in_sem)
        start(loads)
        wait(loads)
        for b in range(cells // BLK):
            here = pl.ds(b * BLK, BLK)
            part = jnp.where(sv[:, here] == 1, 0.5 * pv[b], 0.0)
            for f in range(fields):
                rows_v[f, pl.ds(0, 1), here] = rows_v[f, pl.ds(0, 1), here] + part[f : f + 1]
        stores = copies([(rows_v.at[f], out.at[f, pl.ds(0, 8)]) for f in range(fields)], out_sem)
        start(stores)
        wait(stores)


def finish(ocean_flag, fresh, total, sea):
    fields, olev, cells = fresh.shape
    return pl.pallas_call(
        finish_kernel,
        out_shape=jax.ShapeDtypeStruct(fresh.shape, F32),
        in_specs=[SMEM, HBM, ANY, ANY],
        out_specs=HBM,
        input_output_aliases={1: 0},
        scratch_shapes=[
            pltpu.VMEM(sea.shape, jnp.int32),
            pltpu.VMEM(total.shape, F32),
            pltpu.VMEM((fields, 8, cells), F32),
            pltpu.SemaphoreType.DMA((fields + 2,)),
            pltpu.SemaphoreType.DMA((fields,)),
        ],
        compiler_params=params(8),
        cost_estimate=cost(0, 1 << 16),
        name="finish_ocean",
    )(ocean_flag, fresh, sea, total)


def local(
    atm_state,
    elem_nbr,
    elem_metric,
    bulk_coef,
    stiffness,
    coupling,
    atm_vertical,
    ocean_state,
    cell_nbr,
    cell_diff,
    ocean_vertical,
    sea_mask,
    pair_owner,
    pair_block,
    pair_src,
    remap_weight,
):
    n_comp = lax.axis_size("comp")
    n_dom = lax.axis_size("dom")
    comp_index = lax.axis_index("comp")
    dom_index = lax.axis_index("dom")
    live = n_comp - 1
    chips = n_dom // 2
    state = atm_state[0]
    ocean = ocean_state[0]
    fields, levels, points, elems = state.shape
    cells = ocean.shape[2]
    ocean_blocks = cells // BLK
    one = lambda value: value.astype(jnp.int32).reshape(1)
    flag = one(comp_index == live)
    comp = one(comp_index)
    dom = one(dom_index)
    elem_base = one((comp_index * n_dom + dom_index) * elems)
    cell_base = one(dom_index * cells)

    both = ("comp", "dom")
    swapped = [(d, d ^ 1) for d in range(n_dom)]
    between = [(i, i + 1) for i in range(1, live * n_dom - 1, 2)]
    atm_chips = between + [(j, i) for i, j in between]
    between = [(live * n_dom + i, live * n_dom + i + 1) for i in range(1, n_dom - 1, 2)]
    all_chips = atm_chips + between + [(j, i) for i, j in between]

    def from_ocean(c):
        return [(live * n_dom + d, c * n_dom + d) for d in range(n_dom)]

    def to_ocean(c):
        return [(j, i) for i, j in from_ocean(c)]

    is_ocean = comp_index == live
    chips = n_dom // 2

    def shifted(by):
        return [(d, d ^ (2 * by)) for d in range(n_dom)]

    top = top_rows(flag, ocean)
    brought = [lax.ppermute(top, both, from_ocean(c)) for c in range(live)]
    xt, to_core, to_chip, surface = turn(flag, dom, state, ocean)
    brought, to_core, to_chip = lax.optimization_barrier((brought, to_core, to_chip))
    got = sum(brought)
    got, to_core, to_chip = lax.optimization_barrier((got, to_core, to_chip))
    near = [got] + [lax.ppermute(got, "dom", shifted(s)) for s in range(1, chips)]
    tops = near + [lax.ppermute(part, "dom", swapped) for part in near]
    from_core = lax.ppermute(to_core, "dom", swapped)
    from_chip = lax.ppermute(to_chip, both, all_chips)
    metric = elem_metric[0]

    operators = (elem_nbr[0], coupling.reshape(-1, points), stiffness, metric, atm_vertical)
    flux, sent, fresh = fluxes(
        flag,
        dom,
        pair_owner[0, :, 0],
        pair_block[0],
        pair_src[0],
        tops,
        remap_weight[0],
        bulk_coef[0],
        surface,
        ocean.shape,
        ocean_blocks,
    )
    parts = [lax.ppermute(sent, both, to_ocean(c)) for c in range(live)]
    ue, to_core, to_chip, fresh, zeroed = edge_step(
        flag,
        dom,
        elem_base,
        cell_base,
        xt,
        from_core,
        from_chip,
        *operators,
        flux,
        ocean,
        cell_nbr[0][:, None],
        cell_diff[0][:, None],
        sea_mask,
        ocean_vertical,
        fresh,
    )
    from_chip2 = lax.ppermute(to_chip, both, atm_chips)
    from_core2 = lax.ppermute(to_core, "dom", swapped)
    u, table, xv = inner_step(flag, elem_base, xt, ue, *operators, flux)
    atm_next = second_step(
        flag, dom, xv, u, from_core2, from_chip2, table, metric, atm_vertical, flux, zeroed
    )

    parts, atm_next = lax.optimization_barrier((parts, atm_next))

    def reduce_parts():
        same, other = gather_sent(dom, parts, n_dom)
        pieces = pair_sums(same, lax.ppermute(other, "dom", swapped))
        mine = [pieces[0]]
        for s in range(1, chips):
            mine.append(lax.ppermute(pieces[s], "dom", shifted(s)))
        return add_up(mine)

    total = lax.cond(is_ocean, reduce_parts, lambda: blank((ocean_blocks, fields, BLK)))
    ocean_next = finish(flag, fresh, total, sea_mask)
    return (atm_next.reshape(state.shape)[None], ocean_next[None])


def solution(mesh):
    in_specs = (
        P("comp", None, None, None, "dom"),
        P("comp", None, "dom"),
        P("comp", None, "dom"),
        P("comp", None, "dom"),
        P(),
        P(),
        P(),
        P("comp", None, None, "dom"),
        P("comp", None, "dom"),
        P("comp", None, "dom"),
        P(),
        P("comp", "dom"),
        P("comp", "dom", None),
        P("comp", "dom"),
        P("comp", "dom"),
        P("comp", "dom", None, None),
    )
    out_specs = (P("comp", None, None, None, "dom"), P("comp", None, None, "dom"))
    return jax.shard_map(local, mesh=mesh, in_specs=in_specs, out_specs=out_specs, check_vma=False)
```

```python
import functools

import jax
import jax.numpy as jnp
from jax import lax
from jax.experimental import pallas as pl
from jax.experimental.pallas import tpu as pltpu
from jax.sharding import PartitionSpec as P

RIM = 8
BLK = 128
HALO_O = 128
LANES = 128
GROUP = 8
TURN = 60

F32 = jnp.float32
BF16 = jnp.bfloat16
ANY = pl.BlockSpec(memory_space=pl.ANY)
HBM = pl.BlockSpec(memory_space=pltpu.HBM)
SMEM = pl.BlockSpec(memory_space=pltpu.SMEM)
VMEM = pl.BlockSpec(memory_space=pltpu.VMEM)


def params(mib):
    return pltpu.CompilerParams(vmem_limit_bytes=mib << 20)


def cost(flops, moved):
    return pl.CostEstimate(flops=flops, bytes_accessed=moved, transcendentals=0)


def split(x):
    hi = x.astype(BF16)
    return hi, (x - hi.astype(F32)).astype(BF16)


def dot(a, b):
    return jnp.dot(a, b, preferred_element_type=F32)


def dot_t(a, b):
    return lax.dot_general(a, b, (((1,), (1,)), ((), ())), preferred_element_type=F32)


def turned(rows):
    n = rows.shape[0]
    if n < LANES:
        rows = jnp.concatenate([rows, jnp.zeros((LANES - n, LANES), rows.dtype)], axis=0)
    return rows.T


OCEAN, DOM, ELEM, CELL = range(4)


def copies(pairs, sem):
    return [pltpu.make_async_copy(a, b, sem.at[i]) for i, (a, b) in enumerate(pairs)]


def start(many):
    for one in many:
        one.start()


def wait(many):
    for one in many:
        one.wait()


def hand_out(dom, low_high, to_core, to_chip):
    core = dom[0] % 2
    to_core[...] = low_high[1 - core]
    to_chip[...] = low_high[core]


def take_in(dom, from_core, from_chip, f):
    first = dom[0] % 2 == 0
    a, b = from_core[f], from_chip[f]
    return jnp.where(first, b, a), jnp.where(first, a, b)


def turn_kernel(ocean, dom, x, o, xt, to_core, to_chip, surface, xv, tv, hv, in_sem, out_sem, o_sem):
    fields, points = xv.shape[0], 16
    olev, cells = o.shape[1], o.shape[2]
    groups = LANES // GROUP

    @pl.when(ocean[0] == 0)
    def _():
        loads = copies([(x.at[f], xv.at[f]) for f in range(fields)], in_sem)
        start(loads)
        outs = []
        levels = xv.shape[1] // points
        for f in range(fields):
            loads[f].wait()
            surface[f] = xv[f, pl.ds((levels - 1) * points, points), :]
            hi_at, lo_at = pl.ds(f * LANES, LANES), pl.ds((fields + f) * LANES, LANES)
            for q in range(0, points, 2):
                one = xv[f, pl.ds(q, LANES, stride=points), :].T
                two = xv[f, pl.ds(q + 1, LANES, stride=points), :].T
                for g in range(groups):
                    part = slice(g * GROUP, (g + 1) * GROUP)
                    rows = jnp.concatenate([one[part], two[part]], axis=0)
                    if g == 0:
                        hv[0, f, pl.ds(q * GROUP, 2 * GROUP), :] = rows
                    if g == groups - 1:
                        hv[1, f, pl.ds(q * GROUP, 2 * GROUP), :] = rows
                    hi, lo = split(rows)
                    at = pl.ds((g * points + q) * GROUP, 2 * GROUP)
                    tv[at, hi_at] = hi
                    tv[at, lo_at] = lo
            outs += copies([(tv.at[:, at], xt.at[:, at]) for at in (hi_at, lo_at)], out_sem.at[f])
            start(outs[-2:])
        hand_out(dom, hv, to_core, to_chip)
        wait(outs)

    @pl.when(ocean[0] != 0)
    def _():
        pairs = []
        for f in range(fields):
            pairs.append((o.at[f, :, pl.ds(0, HALO_O)], hv.at[0, f, pl.ds(0, olev)]))
            pairs.append((o.at[f, :, pl.ds(cells - HALO_O, HALO_O)], hv.at[1, f, pl.ds(0, olev)]))
        loads = copies(pairs, o_sem)
        start(loads)
        wait(loads)
        hand_out(dom, hv, to_core, to_chip)


def turn(ocean_flag, dom, state, ocean):
    fields, levels, points, elems = state.shape
    rows = points * elems
    halo = jax.ShapeDtypeStruct((fields, LANES, LANES), F32)
    return pl.pallas_call(
        turn_kernel,
        out_shape=(
            jax.ShapeDtypeStruct((rows, 2 * fields * LANES), BF16),
            halo,
            halo,
            jax.ShapeDtypeStruct((fields, points, elems), F32),
        ),
        in_specs=[SMEM, SMEM, ANY, ANY],
        out_specs=(ANY, VMEM, VMEM, VMEM),
        scratch_shapes=[
            pltpu.VMEM((fields, levels * points, elems), F32),
            pltpu.VMEM((rows, 2 * fields * LANES), BF16),
            pltpu.VMEM((2, fields, LANES, LANES), F32),
            pltpu.SemaphoreType.DMA((fields,)),
            pltpu.SemaphoreType.DMA((fields, 2)),
            pltpu.SemaphoreType.DMA((2 * fields,)),
        ],
        compiler_params=params(TURN),
        cost_estimate=cost(2000000000, 9 << 20),
        name="turn_state",
    )(ocean_flag, dom, state.reshape(fields, levels * points, elems), ocean)


def prepare_table(base, nbr, coupling, stiffness, cx, nt):
    points = stiffness.shape[0]
    nt[...] = turned((nbr[...] - base[0]).astype(F32))
    spread = lax.broadcasted_iota(jnp.int32, (points, LANES), 1) // GROUP
    spread = (spread == lax.broadcasted_iota(jnp.int32, (points, LANES), 0)).astype(F32)
    for ops, first in ((coupling, 0), (stiffness, coupling.shape[0])):
        cx[pl.ds(first, ops.shape[0]), :] = jnp.dot(
            ops[...], spread, precision=lax.Precision.HIGHEST, preferred_element_type=F32
        )


def build_table(block, table, slot, cx, nt, sides, points):
    lane = lax.broadcasted_iota(jnp.int32, (GROUP, LANES), 1) % GROUP
    lane_f = lane.astype(F32)
    same = lane == lax.broadcasted_iota(jnp.int32, (GROUP, LANES), 0)
    zero = jnp.zeros((LANES, LANES), BF16)
    for g in range(2):
        first = pl.multiple_of(block * 2 * GROUP + g * GROUP, GROUP)
        own = nt[pl.ds(first, GROUP), :]
        cols = [jnp.broadcast_to(own[:, s : s + 1], (GROUP, LANES)) for s in range(sides)]
        masks = {}
        for h in range(4):
            if h - g not in (0, 1, 2):
                at = pl.ds(h * LANES, LANES)
                table[slot, pl.ds(g * LANES, LANES), at] = zero
                table[slot, pl.ds((2 + g) * LANES, LANES), at] = zero
                continue
            begin = jnp.asarray(block * 2 * GROUP + (h - 1) * GROUP, jnp.int32).astype(F32)
            masks[h] = [col - begin == lane_f for col in cols]
        for p in range(0, points, 2):
            rows = [
                [jnp.broadcast_to(cx[pl.ds(s * points + pp, 1), :], (GROUP, LANES)) for s in range(sides + 1)]
                for pp in (p, p + 1)
            ]
            for h in masks:
                pair = []
                for row in rows:
                    total = jnp.where(masks[h][0], row[0], 0.0)
                    for s in range(1, sides):
                        total = total + jnp.where(masks[h][s], row[s], 0.0)
                    if h == g + 1:
                        total = total + jnp.where(same, row[sides], 0.0)
                    pair.append(total)
                top, rest = split(jnp.concatenate(pair, axis=0))
                at = pl.ds(h * LANES, LANES)
                table[slot, pl.ds(g * LANES + p * GROUP, 2 * GROUP), at] = top
                table[slot, pl.ds((2 + g) * LANES + p * GROUP, 2 * GROUP), at] = rest


def put_split(xhl, at, f, fields, x):
    hi, lo = split(x)
    xhl[at, pl.ds(f * LANES, LANES)] = hi
    xhl[at, pl.ds((fields + f) * LANES, LANES)] = lo


def columns(turned_rows, first, points):
    pieces = []
    for g in range(2):
        own = turned_rows[pl.ds(pl.multiple_of(first + g * GROUP, GROUP), GROUP), :]
        pieces += [jnp.broadcast_to(own[:, q : q + 1], (GROUP, LANES)) for q in range(points)]
    return jnp.concatenate(pieces, axis=0)


def advance(window, table, wa, mt, element, points, store, chosen):
    fields = window.shape[1] // (2 * LANES)
    rows = 2 * LANES
    n = len(chosen)
    heads = dot(table[...], window[:, pl.ds(chosen[0] * LANES, n * LANES)])
    rest = dot(table[pl.ds(0, rows), :], window[:, pl.ds((fields + chosen[0]) * LANES, n * LANES)])
    inner = pl.ds(LANES, rows)
    hi = [window[inner, f * LANES : (f + 1) * LANES] for f in chosen]
    lo = [window[inner, (fields + f) * LANES : (fields + f + 1) * LANES] for f in chosen]
    v = dot(jnp.concatenate([jnp.concatenate([a, b], axis=1) for a, b in zip(hi, lo)], axis=0), wa[...])
    m = columns(mt, element, points)
    for i, f in enumerate(chosen):
        at = slice(i * LANES, (i + 1) * LANES)
        own = slice(i * rows, (i + 1) * rows)
        tend = heads[:rows, at] + heads[rows:, at] + rest[:, at] + v[own, :LANES] + v[own, LANES:]
        store(f, hi[i].astype(F32) + lo[i].astype(F32) + m * tend)


def prepare(metric, vertical, wa, mt):
    mt[...] = turned(metric[...])
    hi, lo = split(vertical[...].T)
    wa[pl.ds(0, LANES), pl.ds(0, LANES)] = hi
    wa[pl.ds(LANES, LANES), pl.ds(0, LANES)] = hi
    wa[pl.ds(0, LANES), pl.ds(LANES, LANES)] = lo
    wa[pl.ds(LANES, LANES), pl.ds(LANES, LANES)] = jnp.zeros((LANES, LANES), BF16)


def put_flux(ft, flux):
    for f in range(flux.shape[0]):
        ft[f] = turned(-0.5 * flux[f])


def edge_windows(dom, xhl, x, from_core, from_chip):
    fields = from_core.shape[0]
    rows = x.shape[0]
    side = 3 * LANES
    xhl[pl.ds(LANES, side), :] = x[pl.ds(0, side), :]
    xhl[pl.ds(4 * LANES, side), :] = x[pl.ds(rows - side, side), :]
    for f in range(fields):
        left, right = take_in(dom, from_core, from_chip, f)
        put_split(xhl, pl.ds(0, LANES), f, fields, left)
        put_split(xhl, pl.ds(7 * LANES, LANES), f, fields, right)


def edge_kernel(
    ocean, dom, elem, base, xt, from_core, from_chip, enbr, coupling, stiffness, metric, vertical, flux,
    o, nbr, diff, sea, overt, held,
    u, to_core, to_chip, fresh, zeroed,
    table, cx, nt, xhl, hv, wa, mt, ft, ov, ext, res, vert, zv, o_sem, r_sem, z_sem,
):
    del held
    fields, points = flux.shape[0], flux.shape[1]
    blocks = xt.shape[0] // (2 * LANES)
    sides = enbr.shape[0]

    @pl.when(ocean[0] == 0)
    def _():
        prepare_table(elem, enbr, coupling, stiffness, cx, nt)
        for i in range(2):
            build_table(i * (blocks - 1), table, i, cx, nt, sides, points)
        prepare(metric, vertical, wa, mt)
        put_flux(ft, flux)
        edge_windows(dom, xhl, xt, from_core, from_chip)
        last_lane = lax.broadcasted_iota(jnp.int32, (2 * LANES, LANES), 1) == LANES - 1
        for i in range(2):
            b = i * (blocks - 1)
            element = b * 2 * GROUP

            def store(f, value):
                value = value + jnp.where(last_lane, columns(ft.at[f], element, points), 0.0)
                put_split(u, pl.ds(i * 2 * LANES, 2 * LANES), f, fields, value)
                hv[i, f] = value[:LANES] if i == 0 else value[LANES:]

            advance(
                xhl.at[pl.ds(i * 4 * LANES, 4 * LANES)], table.at[i], wa, mt, element, points, store, range(fields)
            )
        hand_out(dom, hv, to_core, to_chip)

    @pl.when(ocean[0] != 0)
    def _():
        load = pltpu.make_async_copy(o, ov, o_sem.at[0])
        load.start()
        zv[...] = jnp.zeros_like(zv)
        zeros = copies([(zv, zeroed.at[f]) for f in range(fields)], z_sem)
        start(zeros)
        ocean_part(dom, base, load, from_core, from_chip, nbr, diff, sea, overt, fresh, ov, ext, res, vert, r_sem)
        wait(zeros)


def edge_step(
    ocean_flag, dom, elem, base, xt, from_core, from_chip, enbr, coupling, stiffness, metric, vertical, flux,
    ocean, nbr, diff, sea, overt, fresh,
):
    width = xt.shape[1]
    points = stiffness.shape[0]
    sides = enbr.shape[0]
    fields = flux.shape[0]
    olev, cells = ocean.shape[1], ocean.shape[2]
    halo = jax.ShapeDtypeStruct((fields, LANES, LANES), F32)
    return pl.pallas_call(
        edge_kernel,
        out_shape=(
            jax.ShapeDtypeStruct((4 * LANES, width), BF16),
            halo,
            halo,
            jax.ShapeDtypeStruct(ocean.shape, F32),
            jax.ShapeDtypeStruct((fields,) + xt.shape[:1] + (LANES,), F32),
        ),
        in_specs=[SMEM] * 4 + [VMEM] * 9 + [HBM] + [VMEM] * 4 + [HBM],
        out_specs=(VMEM, VMEM, VMEM, HBM, HBM),
        input_output_aliases={18: 3},
        scratch_shapes=[
            pltpu.VMEM((2, 4 * LANES, 4 * LANES), BF16),
            pltpu.VMEM(((sides + 1) * points, LANES), F32),
            pltpu.VMEM((LANES, LANES), F32),
            pltpu.VMEM((8 * LANES, width), BF16),
            pltpu.VMEM((2, fields, LANES, LANES), F32),
            pltpu.VMEM((2 * LANES, 2 * LANES), BF16),
            pltpu.VMEM((LANES, LANES), F32),
            pltpu.VMEM((fields, LANES, LANES), F32),
            pltpu.VMEM(ocean.shape, F32),
            pltpu.VMEM((2, fields * olev, cells + 2 * HALO_O), BF16),
            pltpu.VMEM(ocean.shape, F32),
            pltpu.VMEM(ocean.shape, F32),
            pltpu.VMEM(xt.shape[:1] + (LANES,), F32),
            pltpu.SemaphoreType.DMA((1,)),
            pltpu.SemaphoreType.DMA((1,)),
            pltpu.SemaphoreType.DMA((fields,)),
        ],
        compiler_params=params(20),
        cost_estimate=cost(4000000000, 3 << 20),
        name="edge_step",
    )(
        ocean_flag, dom, elem, base, xt, from_core, from_chip, enbr, coupling, stiffness, metric, vertical, flux,
        ocean, nbr, diff, sea, overt, fresh,
    )


def inner_kernel(ocean, elem, xt, ue, enbr, coupling, stiffness, metric, vertical, flux, u, table, xv, cx, nt, wa, mt, ft):
    fields, points = flux.shape[0], flux.shape[1]
    sides = enbr.shape[0]
    rows = xt.shape[0]
    blocks = table.shape[0]
    edge = 2 * LANES

    @pl.when(ocean[0] == 0)
    def _():
        prepare_table(elem, enbr, coupling, stiffness, cx, nt)
        for b in range(2):
            build_table(b, table, b, cx, nt, sides, points)
        prepare(metric, vertical, wa, mt)
        put_flux(ft, flux)
        u[pl.ds(0, edge), :] = ue[pl.ds(0, edge), :]
        u[pl.ds(rows - edge, edge), :] = ue[pl.ds(edge, edge), :]
        last_lane = lax.broadcasted_iota(jnp.int32, (edge, LANES), 1) == LANES - 1

        for b in range(1, blocks - 1):
            element = b * 2 * GROUP

            def store(f, value):
                value = value + jnp.where(last_lane, columns(ft.at[f], element, points), 0.0)
                put_split(u, pl.ds(b * edge, edge), f, fields, value)

            build_table(b + 1, table, b + 1, cx, nt, sides, points)
            window = xt.at[pl.ds(b * edge - LANES, 4 * LANES)]
            advance(window, table.at[b], wa, mt, element, points, store, range(fields))

        for b in range(1, blocks - 1):

            def store(f, value):
                xv[f, pl.ds(b * edge, edge), :] = value

            window = u.at[pl.ds(b * edge - LANES, 4 * LANES)]
            advance(window, table.at[b], wa, mt, b * 2 * GROUP, points, store, range(fields))


def ocean_part(dom, base, load, from_core, from_chip, nbr, diff, sea, overt, fresh, ov, ext, res, vert, r_sem):
    fields, olev, cells = ov.shape
    sides = nbr.shape[0]
    for f in range(fields):
        rows = pl.ds(f * olev, olev)
        left, right = take_in(dom, from_core, from_chip, f)
        for at, value in ((0, left[:olev]), (HALO_O + cells, right[:olev])):
            hi, lo = split(value)
            ext[0, rows, pl.ds(at, HALO_O)] = hi
            ext[1, rows, pl.ds(at, HALO_O)] = lo
    vhi, vlo = split(overt[...])
    both = jnp.concatenate([vhi, vlo], axis=0)
    load.wait()
    for f in range(fields):
        rows = pl.ds(f * olev, olev)
        hi, lo = split(ov[f])
        ext[0, rows, pl.ds(HALO_O, cells)] = hi
        ext[1, rows, pl.ds(HALO_O, cells)] = lo
        v = dot(both, hi)
        vert[f] = v[:olev] + v[olev:] + dot(vhi, lo)

    @pl.loop(0, cells // LANES)
    def _(b):
        first = pl.multiple_of(b * LANES, LANES)
        here = pl.ds(first, LANES)
        begin = base[0] + first - HALO_O
        place = lax.broadcasted_iota(jnp.int32, (3 * LANES, LANES), 0)
        table = jnp.zeros((3 * LANES, LANES), F32)
        held = jnp.zeros((1, LANES), F32)
        for k in range(sides):
            d = diff[k, :, here]
            held = held + d
            table = table + jnp.where(place == nbr[k, :, here] - begin, d, 0.0)
        hi, lo = split(table)
        window = pl.ds(first, 3 * LANES)
        heads = dot(ext[0, :, window], jnp.concatenate([hi, lo], axis=1))
        lap = heads[:, :LANES] + heads[:, LANES:] + dot(ext[1, :, window], hi)
        wet = sea[:, here] == 1
        for f in range(fields):
            own = ov[f, :, here]
            new = own + (lap[f * olev : (f + 1) * olev] - held * own) + vert[f, :, here]
            res[f, :, here] = jnp.where(wet, new, own)

    out = pltpu.make_async_copy(res, fresh, r_sem.at[0])
    out.start()
    out.wait()


def inner_step(ocean_flag, elem, xt, ue, enbr, coupling, stiffness, metric, vertical, flux):
    rows, width = xt.shape
    fields, points = flux.shape[0], flux.shape[1]
    sides = enbr.shape[0]
    blocks = rows // (2 * LANES)
    return pl.pallas_call(
        inner_kernel,
        out_shape=(
            jax.ShapeDtypeStruct((rows, width), BF16),
            jax.ShapeDtypeStruct((blocks, 4 * LANES, 4 * LANES), BF16),
            jax.ShapeDtypeStruct((fields, rows, LANES), F32),
        ),
        in_specs=[SMEM, SMEM] + [VMEM] * 8,
        out_specs=(VMEM, VMEM, VMEM),
        scratch_shapes=[
            pltpu.VMEM(((sides + 1) * points, LANES), F32),
            pltpu.VMEM((LANES, LANES), F32),
            pltpu.VMEM((2 * LANES, 2 * LANES), BF16),
            pltpu.VMEM((LANES, LANES), F32),
            pltpu.VMEM((fields, LANES, LANES), F32),
        ],
        compiler_params=params(12),
        cost_estimate=cost(10_000_000_000, 10 << 20),
        name="inner_step",
    )(ocean_flag, elem, xt, ue, enbr, coupling, stiffness, metric, vertical, flux)


def flux_kernel(ocean, dom, owner, block, source, *refs):
    n_tops = len(refs) - 14
    tops = refs[:n_tops]
    weights, coef, surface, flux, sent, fresh, sv, tv, wcat, surf, fl, zv, z_sem, s_sem = refs[n_tops:]
    pairs = weights.shape[0]
    points, fields = coef.shape[0], flux.shape[0]
    ocean_blocks = sent.shape[0] // n_tops
    chips = n_tops // 2

    @pl.when(ocean[0] == 0)
    def _():
        load = pltpu.make_async_copy(surface, sv, s_sem)
        load.start()
        zv[...] = jnp.zeros_like(zv)
        zeros = copies([(zv, fresh.at[f]) for f in range(fields)], z_sem)
        start(zeros)
        surf[...] = jnp.zeros_like(surf)
        sent[...] = jnp.zeros_like(sent)
        chip, core = dom[0] // 2, dom[0] % 2

        def doubled(rows):
            hi, lo = split(rows)
            eight = jnp.concatenate([hi.astype(F32), lo.astype(F32)], axis=0).astype(BF16)
            return jnp.concatenate([eight, eight], axis=1)

        @pl.loop(0, pairs, unroll=4)
        def _(r):
            hi, lo = split(weights[r])
            wcat[r, :, pl.ds(0, BLK)] = hi
            wcat[r, :, pl.ds(BLK, BLK)] = lo

        for i in range(n_tops):
            tv[i] = tops[i][...]
        for r in range(pairs):
            at = pl.multiple_of(block[r] * BLK, BLK)
            which = owner[r]
            slot = ((which // 2) ^ chip) + jnp.where(which % 2 == core, 0, chips)
            rows = doubled(tv[slot, :, pl.ds(at, BLK)])
            out = dot_t(rows, wcat[r])
            surf[source[r]] += out[:fields] + out[fields:]

        load.wait()
        for p in range(points):
            value = coef[pl.ds(p, 1), :] * (sv[:, p, :] - surf[p])
            fl[p] = value
            flux[:, p, :] = value

        for r in range(pairs):
            rows = doubled(fl[source[r]])
            both = jnp.concatenate([wcat[r, :, pl.ds(0, BLK)], wcat[r, :, pl.ds(BLK, BLK)]], axis=0)
            out = dot(rows, both)
            sent[owner[r] * ocean_blocks + block[r]] += out[:fields] + out[fields:]
        wait(zeros)


def fluxes(ocean_flag, dom, owner, block, source, tops, weights, coef, surface, ocean_shape, ocean_blocks):
    fields, points, elems = surface.shape
    pairs = weights.shape[0]
    n = len(tops)
    return pl.pallas_call(
        flux_kernel,
        out_shape=(
            jax.ShapeDtypeStruct((fields, points, elems), F32),
            jax.ShapeDtypeStruct((n * ocean_blocks, fields, BLK), F32),
            jax.ShapeDtypeStruct(ocean_shape, F32),
        ),
        in_specs=[SMEM] * 5 + [VMEM] * (n + 2) + [ANY],
        out_specs=(VMEM, VMEM, HBM),
        scratch_shapes=[
            pltpu.VMEM((fields, points, elems), F32),
            pltpu.VMEM((n,) + tops[0].shape, F32),
            pltpu.VMEM((pairs, BLK, 2 * BLK), BF16),
            pltpu.VMEM((points, fields, BLK), F32),
            pltpu.VMEM((points, fields, BLK), F32),
            pltpu.VMEM(ocean_shape[1:], F32),
            pltpu.SemaphoreType.DMA((fields,)),
            pltpu.SemaphoreType.DMA,
        ],
        compiler_params=params(8),
        cost_estimate=cost(2_500_000_000, 2 << 20),
        name="fluxes",
    )(ocean_flag, dom, owner, block, source, *tops, weights, coef, surface)


def second_kernel(
    ocean, dom, xv, u, from_core, from_chip, table, metric, vertical, flux, held, out, xhl, wa, mt, xe, ov, o_sem
):
    del held
    fields, points = flux.shape[0], flux.shape[1]
    blocks = table.shape[0]
    levels = xv.shape[2]
    groups = LANES // GROUP
    edge = 2 * LANES

    @pl.when(ocean[0] == 0)
    def _():
        prepare(metric, vertical, wa, mt)
        edge_windows(dom, xhl, u, from_core, from_chip)
        for i in range(2):
            b = i * (blocks - 1)

            def store(f, value):
                xe[f, pl.ds(i * edge, edge), :] = value

            advance(
                xhl.at[pl.ds(i * 4 * LANES, 4 * LANES)], table.at[b], wa, mt, b * 2 * GROUP, points, store, range(fields)
            )
        outs = copies([(ov.at[f], out.at[f]) for f in range(fields)], o_sem)
        for f in range(fields):
            for p in range(points):
                cols = []
                for g in range(groups):
                    if 2 <= g < groups - 2:
                        cols.append(xv[f, pl.ds(g * LANES + p * GROUP, GROUP), :])
                    else:
                        cols.append(xe[f, pl.ds((g % (groups - 4)) * LANES + p * GROUP, GROUP), :])
                ov[f, pl.ds(p, LANES, stride=points), :] = jnp.concatenate(cols, axis=0).T
            last = pl.ds((levels - 1) * points, points)
            ov[f, last, :] = ov[f, last, :] - 0.5 * flux[f]
            outs[f].start()
        wait(outs)


def second_step(ocean_flag, dom, xv, u, from_core, from_chip, table, metric, vertical, flux, zeroed):
    fields, rows, levels = xv.shape
    points = flux.shape[1]
    width = u.shape[1]
    return pl.pallas_call(
        second_kernel,
        out_shape=jax.ShapeDtypeStruct((fields, levels * points, LANES), F32),
        in_specs=[SMEM, SMEM] + [VMEM] * 8 + [HBM],
        out_specs=HBM,
        input_output_aliases={10: 0},
        scratch_shapes=[
            pltpu.VMEM((8 * LANES, width), BF16),
            pltpu.VMEM((2 * LANES, 2 * LANES), BF16),
            pltpu.VMEM((LANES, LANES), F32),
            pltpu.VMEM((fields, 4 * LANES, levels), F32),
            pltpu.VMEM((fields, levels * points, LANES), F32),
            pltpu.SemaphoreType.DMA((fields,)),
        ],
        compiler_params=params(20),
        cost_estimate=cost(10_000_000_000, 12 << 20),
        name="second_step",
    )(ocean_flag, dom, xv, u, from_core, from_chip, table, metric, vertical, flux, zeroed)


def blank_kernel(out):
    del out


def blank(shape):
    return pl.pallas_call(
        blank_kernel, out_shape=jax.ShapeDtypeStruct(shape, F32), out_specs=HBM, compiler_params=params(4), cost_estimate=cost(0, 1024), name="blank"
    )()


def top_kernel(ocean, o, top, tv, sem):
    fields = top.shape[0]

    @pl.when(ocean[0] != 0)
    def _():
        loads = copies([(o.at[f, pl.ds(0, 8)], tv.at[f]) for f in range(fields)], sem)
        start(loads)
        wait(loads)
        for f in range(fields):
            top[pl.ds(f, 1), :] = tv[f, pl.ds(0, 1), :]


def top_rows(ocean_flag, ocean):
    fields, olev, cells = ocean.shape
    return pl.pallas_call(
        top_kernel,
        out_shape=jax.ShapeDtypeStruct((fields, cells), F32),
        in_specs=[SMEM, ANY],
        out_specs=VMEM,
        scratch_shapes=[pltpu.VMEM((fields, 8, cells), F32), pltpu.SemaphoreType.DMA((fields,))],
        compiler_params=params(TURN),
        cost_estimate=cost(0, 1 << 16),
        name="top_rows",
    )(ocean_flag, ocean)


def gather_kernel(dom, *refs):
    parts, (keep, give) = refs[:-2], refs[-2:]
    half, per = keep.shape[0], keep.shape[1]
    for core, out in ((0, keep), (1, give)):
        for s in range(half):
            at = pl.ds((dom[0] ^ (2 * s + core)) * per, per)
            total = parts[0][at]
            for part in parts[1:]:
                total = total + part[at]
            out[s] = total


def gather_sent(dom, parts, n_dom):
    total, fields, blk = parts[0].shape
    shape = jax.ShapeDtypeStruct((n_dom // 2, total // n_dom, fields, blk), F32)
    return pl.pallas_call(
        gather_kernel,
        out_shape=(shape, shape),
        in_specs=[SMEM] + [VMEM] * len(parts),
        out_specs=(VMEM, VMEM),
        compiler_params=params(6),
        name="gather_sent",
    )(dom, *parts)


def pair_kernel(same, other, *outs):
    for s, out in enumerate(outs):
        out[...] = same[s] + other[s]


def pair_sums(same, other):
    chips = same.shape[0]
    return pl.pallas_call(
        pair_kernel,
        out_shape=(jax.ShapeDtypeStruct(same.shape[1:], F32),) * chips,
        in_specs=[VMEM, VMEM],
        out_specs=(VMEM,) * chips,
        compiler_params=params(4),
        cost_estimate=cost(0, 1 << 16),
        name="pair_sums",
    )(same, other)


def add_kernel(*refs):
    parts, out = refs[:-1], refs[-1]
    total = parts[0][...]
    for part in parts[1:]:
        total = total + part[...]
    out[...] = total


def add_up(parts):
    return pl.pallas_call(
        add_kernel,
        out_shape=jax.ShapeDtypeStruct(parts[0].shape, F32),
        in_specs=[VMEM] * len(parts),
        out_specs=VMEM,
        compiler_params=params(4),
        cost_estimate=cost(0, 1 << 16),
        name="add_up",
    )(*parts)


def finish_kernel(ocean, fresh, sea, total, out, sv, pv, rows_v, in_sem, out_sem):
    del fresh
    fields, cells = rows_v.shape[0], rows_v.shape[2]

    @pl.when(ocean[0] != 0)
    def _():
        loads = copies([(out.at[f, pl.ds(0, 8)], rows_v.at[f]) for f in range(fields)] + [(total, pv), (sea, sv)], in_sem)
        start(loads)
        wait(loads)
        for b in range(cells // BLK):
            here = pl.ds(b * BLK, BLK)
            part = jnp.where(sv[:, here] == 1, 0.5 * pv[b], 0.0)
            for f in range(fields):
                rows_v[f, pl.ds(0, 1), here] = rows_v[f, pl.ds(0, 1), here] + part[f : f + 1]
        stores = copies([(rows_v.at[f], out.at[f, pl.ds(0, 8)]) for f in range(fields)], out_sem)
        start(stores)
        wait(stores)


def finish(ocean_flag, fresh, total, sea):
    fields, olev, cells = fresh.shape
    return pl.pallas_call(
        finish_kernel,
        out_shape=jax.ShapeDtypeStruct(fresh.shape, F32),
        in_specs=[SMEM, HBM, ANY, ANY],
        out_specs=HBM,
        input_output_aliases={1: 0},
        scratch_shapes=[
            pltpu.VMEM(sea.shape, jnp.int32),
            pltpu.VMEM(total.shape, F32),
            pltpu.VMEM((fields, 8, cells), F32),
            pltpu.SemaphoreType.DMA((fields + 2,)),
            pltpu.SemaphoreType.DMA((fields,)),
        ],
        compiler_params=params(8),
        cost_estimate=cost(0, 1 << 16),
        name="finish_ocean",
    )(ocean_flag, fresh, sea, total)


def local(
    atm_state,
    elem_nbr,
    elem_metric,
    bulk_coef,
    stiffness,
    coupling,
    atm_vertical,
    ocean_state,
    cell_nbr,
    cell_diff,
    ocean_vertical,
    sea_mask,
    pair_owner,
    pair_block,
    pair_src,
    remap_weight,
):
    n_comp = lax.axis_size("comp")
    n_dom = lax.axis_size("dom")
    comp_index = lax.axis_index("comp")
    dom_index = lax.axis_index("dom")
    live = n_comp - 1
    chips = n_dom // 2
    state = atm_state[0]
    ocean = ocean_state[0]
    fields, levels, points, elems = state.shape
    cells = ocean.shape[2]
    ocean_blocks = cells // BLK
    one = lambda value: value.astype(jnp.int32).reshape(1)
    flag = one(comp_index == live)
    comp = one(comp_index)
    dom = one(dom_index)
    elem_base = one((comp_index * n_dom + dom_index) * elems)
    cell_base = one(dom_index * cells)

    both = ("comp", "dom")
    swapped = [(d, d ^ 1) for d in range(n_dom)]
    between = [(i, i + 1) for i in range(1, live * n_dom - 1, 2)]
    atm_chips = between + [(j, i) for i, j in between]
    between = [(live * n_dom + i, live * n_dom + i + 1) for i in range(1, n_dom - 1, 2)]
    all_chips = atm_chips + between + [(j, i) for i, j in between]

    def from_ocean(c):
        return [(live * n_dom + d, c * n_dom + d) for d in range(n_dom)]

    def to_ocean(c):
        return [(j, i) for i, j in from_ocean(c)]

    is_ocean = comp_index == live
    chips = n_dom // 2

    def shifted(by):
        return [(d, d ^ (2 * by)) for d in range(n_dom)]

    top = top_rows(flag, ocean)
    brought = [lax.ppermute(top, both, from_ocean(c)) for c in range(live)]
    xt, to_core, to_chip, surface = turn(flag, dom, state, ocean)
    brought, to_core, to_chip = lax.optimization_barrier((brought, to_core, to_chip))
    got = sum(brought)
    got, to_core, to_chip = lax.optimization_barrier((got, to_core, to_chip))
    near = [got] + [lax.ppermute(got, "dom", shifted(s)) for s in range(1, chips)]
    tops = near + [lax.ppermute(part, "dom", swapped) for part in near]
    from_core = lax.ppermute(to_core, "dom", swapped)
    from_chip = lax.ppermute(to_chip, both, all_chips)
    metric = elem_metric[0]

    operators = (elem_nbr[0], coupling.reshape(-1, points), stiffness, metric, atm_vertical)
    flux, sent, fresh = fluxes(
        flag,
        dom,
        pair_owner[0, :, 0],
        pair_block[0],
        pair_src[0],
        tops,
        remap_weight[0],
        bulk_coef[0],
        surface,
        ocean.shape,
        ocean_blocks,
    )
    parts = [lax.ppermute(sent, both, to_ocean(c)) for c in range(live)]
    ue, to_core, to_chip, fresh, zeroed = edge_step(
        flag,
        dom,
        elem_base,
        cell_base,
        xt,
        from_core,
        from_chip,
        *operators,
        flux,
        ocean,
        cell_nbr[0][:, None],
        cell_diff[0][:, None],
        sea_mask,
        ocean_vertical,
        fresh,
    )
    from_chip2 = lax.ppermute(to_chip, both, atm_chips)
    from_core2 = lax.ppermute(to_core, "dom", swapped)
    u, table, xv = inner_step(flag, elem_base, xt, ue, *operators, flux)
    atm_next = second_step(
        flag, dom, xv, u, from_core2, from_chip2, table, metric, atm_vertical, flux, zeroed
    )

    parts, atm_next = lax.optimization_barrier((parts, atm_next))

    def reduce_parts():
        same, other = gather_sent(dom, parts, n_dom)
        pieces = pair_sums(same, lax.ppermute(other, "dom", swapped))
        mine = [pieces[0]]
        for s in range(1, chips):
            mine.append(lax.ppermute(pieces[s], "dom", shifted(s)))
        return add_up(mine)

    total = lax.cond(is_ocean, reduce_parts, lambda: blank((ocean_blocks, fields, BLK)))
    ocean_next = finish(flag, fresh, total, sea_mask)
    return (atm_next.reshape(state.shape)[None], ocean_next[None])


def solution(mesh):
    in_specs = (
        P("comp", None, None, None, "dom"),
        P("comp", None, "dom"),
        P("comp", None, "dom"),
        P("comp", None, "dom"),
        P(),
        P(),
        P(),
        P("comp", None, None, "dom"),
        P("comp", None, "dom"),
        P("comp", None, "dom"),
        P(),
        P("comp", "dom"),
        P("comp", "dom", None),
        P("comp", "dom"),
        P("comp", "dom"),
        P("comp", "dom", None, None),
    )
    out_specs = (P("comp", None, None, None, "dom"), P("comp", None, None, "dom"))
    return jax.shard_map(local, mesh=mesh, in_specs=in_specs, out_specs=out_specs, check_vma=False)
```
